256 devices in a mesh: seq: 32 (over y, z), head: 8 (over x, core).
Axes of the slice: x: 4, y: 4, z: 8, core: 2. Of those that a mesh axis runs over, the one named last changes fastest.
Arguments:
- queries: bfloat16 [128, 16, 4096], P('seq', None, 'head'), may hold values from -6 to 6
- incoming_key_value: bfloat16 [2, 128, 16, 2048], P(None, 'seq', None, 'head'), may hold values from -6 to 6
- prefix_key_value_pool: bfloat16 [2, 256, 512, 2048], P(None, 'seq', None, 'head'), may hold values from -6 to 6
- response_key_value: bfloat16 [2, 128, 2048, 2048], P(None, 'seq', None, 'head'), may hold values from -6 to 6
- residual: bfloat16 [128, 16, 4608], P('seq', None, 'head')
- lengths: int32 [128], P('seq'), may hold values from 1 to 2048, 131072 in all
- rollout_task_map: int32 [128, 1], replicated, may hold values from 0 to 11; in each aligned block of 128 rows (0 to 127, 128 to 255, ...) at most 22 rows name the same one
- slot_block_table: int32 [256], P('seq'), may hold values from 0 to 255, each once
- output_projection_weight: bfloat16 [4096, 4608], P('head'), may hold values from -0.125 to 0.125
- adapter_down_weight: bfloat16 [4096, 16], P('head'), may hold values from -0.09375 to 0.09375
- adapter_up_weight: bfloat16 [16, 4608], replicated, may hold values from -1.5 to 1.5
- post_norm_gain: float32 [4608], P('head'), may hold values from 0.5 to 1.5
- value_head_weight: float32 [4608], P('head'), may hold values from -0.09375 to 0.09375
Outputs:
- hidden: bfloat16 [128, 16, 4608], P('seq', None, 'head')
- values: float32 [128, 16], P('seq')
The draws below stay inside these ranges and needn't reach their ends.
Inputs may be any that keep to these rules, and one draw needn't show every extreme that they name: `rollout_task_map`: each task prompt is the prompt of at least one and at most 22 rollouts; some prompt has exactly 22. `lengths`: the largest length is exactly 2048. `slot_block_table`: a permutation; blocks below 64 are the system context, block 64 + p * 16 + j is block j of task prompt p.
All inputs are finite; a program needn't handle non-finite values. No bound on the sum of `lengths` on one device may be relied on, other than what follows from the above.
Results may differ from the reference program's by a relative error of at most 0.0054.
Values may be sent and summed in bfloat16 or wider, within the bound.
A program may use at most 128 MiB of HBM per device.

```python
import math
import jax
import jax.numpy as jnp
import numpy as np
from jax import lax

MODEL_WIDTH = 4608
QUERY_HEADS = 32
KV_HEADS = 16
HEAD_SIZE = 128
ADAPTER_RANK = 16
NEW = 16
RMAX = 2048
BLK = 512
PROMPT_BLOCKS = 16
ROLLOUTS = 128
SYS_BLOCKS = 64
PROMPTS = 12
PBLOCKS = 256
CAP = 22


def draw_residual(key, part):
    key = jax.random.fold_in(key, 11)
    first, second, third = jax.random.split(key, 3)
    columns = jnp.arange(MODEL_WIDTH, dtype=jnp.float32) / MODEL_WIDTH
    spread = 2.0 ** jax.random.uniform(second, (MODEL_WIDTH,), jnp.float32)
    base = jax.random.normal(first, (ROLLOUTS, NEW, MODEL_WIDTH), jnp.float32)
    row_scale = 1.0 + 0.0 * jax.random.uniform(third, (ROLLOUTS, NEW, 1), jnp.float32)
    return (base * row_scale * spread * 0.2 * 3.0 ** columns).astype(jnp.bfloat16)


def strengthened(array, rng, source, target, blocks, factor):
    def block_of(dim):
        return (jnp.arange(array.shape[dim]) // (array.shape[dim] // blocks)).reshape((-1,) + (1,) * (array.ndim - 1 - dim))

    first = jax.random.permutation(rng, blocks)[block_of(target)]
    other_side = (block_of(target) + blocks // 2) % blocks
    return jnp.where((block_of(source) == first) | (block_of(source) == other_side), factor * array, array)


def block_scale(rng, extent, pieces, least, top_value):
    def one(axis_at, blocks):
        steps = jax.random.uniform(jax.random.fold_in(jax.random.fold_in(rng, 6), axis_at), (blocks,), jnp.float32, least / len(pieces), top_value / len(pieces))
        return jnp.repeat(jnp.exp(steps), extent[axis_at] // blocks).reshape((-1,) + (1,) * (len(extent) - axis_at - 1))

    factor_of = one(*pieces[0])
    for cut in pieces[1:]:
        factor_of = factor_of * one(*cut)
    return factor_of


def length_profile(number_of, total, bound, lean):
    loads = [(1 << 20) // math.isqrt(grade ** lean) + 1 for grade in range(2, number_of + 1)]
    surplus, given = total - bound - (number_of - 1), [1] * (number_of - 1)
    while surplus > 0:
        movable = [i for i in range(number_of - 1) if given[i] < bound]
        whole, budget = sum([loads[i] for i in movable]), surplus
        for i in movable:
            extra = min(bound - given[i], max(1, budget * loads[i] // whole), surplus)
            given[i] = given[i] + extra
            surplus = surplus - extra
    return np.array([bound] + given)


def ragged(rng, number_of, total, most, skew):
    if number_of == 2:
        one = jax.random.randint(rng, (), max(1, total - most), min(most, total - 1) + 1)
        return jnp.stack([one, total - one])
    sizes = jnp.asarray(length_profile(number_of, total, most, skew), jnp.int32)
    pairs = (number_of - 1) // 2
    donor, receiver = sizes[1:1 + 2 * pairs:2], sizes[2:2 + 2 * pairs:2]
    room = jnp.minimum(donor - 1, most - receiver)
    shifted = jax.random.randint(jax.random.fold_in(rng, 1), (pairs,), 0, 1 << 20) % (room + 1)
    sizes = sizes.at[1:1 + 2 * pairs:2].set(donor - shifted).at[2:2 + 2 * pairs:2].set(receiver + shifted)
    return sizes[jax.random.permutation(jax.random.fold_in(rng, 2), number_of)]


def deal_out(own_key, own, number, rows, number_of, top, most, lean):
    order = jax.random.permutation(own_key, number_of)
    crowded, common = shares(number_of, rows * top, most, lean, True), shares(number_of, rows * top, most, lean, False)
    places = jnp.arange(number_of)

    def named(sizes, offset_by):
        used = int((sizes > 0).sum())
        fixed = max(1, used // 4)
        passed = fixed + (places - fixed + offset_by * (used - fixed)) % max(1, number_of - fixed)
        return jnp.zeros((number_of,), jnp.int32).at[order[jnp.where(places < fixed, places, passed)]].set(jnp.asarray(sizes, jnp.int32))

    sizes = jnp.where(number % 4 == 0, named(crowded, number // 4), named(common, number - number // 4 - 1))
    mixed = jax.random.permutation(jax.random.fold_in(own, 3), number_of)
    source_of, sink = mixed[0:number_of // 2 * 2:2], mixed[1:number_of // 2 * 2:2]
    margin = jnp.minimum(sizes[source_of] - 1, most - sizes[sink]) // 2
    margin = jnp.where((source_of == order[0]) | (sink == order[0]) | (sizes[sink] == 0), 0, jnp.maximum(margin, 0))
    passed = jax.random.randint(jax.random.fold_in(own, 4), (number_of // 2,), 0, 1 << 20) % (margin + 1)
    sizes = sizes.at[source_of].add(-passed).at[sink].add(passed)
    labels = jnp.searchsorted(jnp.cumsum(sizes), jnp.arange(rows * top), side="right").astype(jnp.int32)
    grid = labels.reshape(top, rows).T
    grid = grid[jax.random.permutation(jax.random.fold_in(own, 1), rows)]
    offset_by = jax.random.randint(jax.random.fold_in(own, 2), (rows, 1), 0, top)
    return jnp.take_along_axis(grid, (jnp.arange(top)[None, :] + offset_by) % top, axis=1)


def shares(count, total, limit, lean, full):
    loads = [(1 << 20) // math.isqrt(grade ** lean) + 1 for grade in range(1, count + 1)]
    largest = limit if full else min(limit, max(-(-total // count), total * loads[0] // sum(loads)))
    least = 1 if total - largest >= count - 1 else 0
    counts, spare = [largest] + [least] * (count - 1), total - largest - least * (count - 1)
    while spare > 0:
        candidates = [i for i in range(1, count) if counts[i] < largest] or [i for i in range(1, count) if counts[i] < limit]
        mass, left = sum([loads[i] for i in candidates]), spare
        for i in candidates:
            addition = min(limit - counts[i], max(1, left * loads[i] // mass), spare)
            counts[i] = counts[i] + addition
            spare = spare - addition
    return np.array(counts)


def bell_draw(key, extent, deviation, reach, shards=(), held_as=jnp.bfloat16):
    result = jax.random.normal(key, extent, jnp.float32) * deviation
    if len(shards) > 0:
        result = block_scale(key, extent, shards, -0.22, 0.18) * result
    return jnp.clip(result, min=-reach, max=reach).astype(held_as)


def gaussian_with(own_key, dims, width, bound, cuts, heavy, kind=jnp.bfloat16):
    drawn = width * jax.random.normal(own_key, dims, jnp.float32)
    if cuts:
        drawn = drawn * block_scale(own_key, dims, cuts, -0.22, 0.18)
    return jnp.clip(strengthened(drawn, jax.random.fold_in(own_key, 3), *heavy), -bound, bound).astype(kind)


def setup_inputs(seed: int = 0) -> dict:
    splits = jax.random.split(jax.random.key(seed), 14)
    queries = bell_draw(splits[0], (ROLLOUTS, NEW, QUERY_HEADS * HEAD_SIZE), 1.0, 6.0, ((0, 32), (2, 8)))
    incoming_key_value = bell_draw(splits[1], (2, ROLLOUTS, NEW, KV_HEADS * HEAD_SIZE), 1.0, 6.0, ((1, 32), (3, 8)))
    prefix_key_value_pool = bell_draw(splits[2], (2, PBLOCKS, BLK, KV_HEADS * HEAD_SIZE), 1.0, 6.0, ((1, 32), (3, 8)))
    response_key_value = bell_draw(splits[3], (2, ROLLOUTS, RMAX, KV_HEADS * HEAD_SIZE), 1.0, 6.0, ((1, 32), (3, 8)))
    residual = draw_residual(jax.random.fold_in(splits[13], 71), 0)
    lengths = ragged(splits[5], ROLLOUTS, ROLLOUTS * RMAX // 2, RMAX, 2).astype(jnp.int32)
    rollout_task_map_keys = jax.random.split(jax.random.fold_in(splits[6], 1), ROLLOUTS // ROLLOUTS)
    rollout_task_map_turns = jax.random.permutation(jax.random.fold_in(splits[6], 3), ROLLOUTS // ROLLOUTS)
    rollout_task_map = jax.vmap(lambda own, number: deal_out(jax.random.fold_in(splits[6], 2), own, number, ROLLOUTS, PROMPTS, 1, CAP, 2))(rollout_task_map_keys, rollout_task_map_turns).reshape((ROLLOUTS, 1))
    slot_block_table = jax.random.permutation(splits[7], PBLOCKS).astype(jnp.int32)
    output_projection_weight = gaussian_with(splits[8], (QUERY_HEADS * HEAD_SIZE, MODEL_WIDTH), (QUERY_HEADS * HEAD_SIZE) ** -0.5, 0.125, ((0, 8),), (0, 1, 8, 2.0))
    adapter_down_weight = bell_draw(splits[9], (QUERY_HEADS * HEAD_SIZE, ADAPTER_RANK), (QUERY_HEADS * HEAD_SIZE) ** -0.5, 0.09375, ((0, 8),))
    adapter_up_weight = bell_draw(splits[10], (ADAPTER_RANK, MODEL_WIDTH), ADAPTER_RANK ** -0.5, 1.5)
    post_norm_gain = jnp.clip(1.0 + 0.1 * jax.random.normal(splits[11], (MODEL_WIDTH,), jnp.float32), 0.5, 1.5)
    value_head_weight = bell_draw(splits[12], (MODEL_WIDTH,), MODEL_WIDTH ** -0.5, 0.09375, ((0, 8),), jnp.float32)
    return {"queries": queries, "incoming_key_value": incoming_key_value, "prefix_key_value_pool": prefix_key_value_pool, "response_key_value": response_key_value, "residual": residual, "lengths": lengths, "rollout_task_map": rollout_task_map, "slot_block_table": slot_block_table, "output_projection_weight": output_projection_weight, "adapter_down_weight": adapter_down_weight, "adapter_up_weight": adapter_up_weight, "post_norm_gain": post_norm_gain, "value_head_weight": value_head_weight}


SCALE = 144.0 ** (-0.5)
SOFTCAP = 50.0
EPS = 1e-06

def reference(queries, incoming_key_value, prefix_key_value_pool, response_key_value, residual, lengths, rollout_task_map, slot_block_table, output_projection_weight, adapter_down_weight, adapter_up_weight, post_norm_gain, value_head_weight):
    slot_of = jnp.zeros((PBLOCKS,), jnp.int32).at[slot_block_table].set(jnp.arange(PBLOCKS, dtype=jnp.int32))
    per_group = QUERY_HEADS // KV_HEADS
    prefix_count = (SYS_BLOCKS + PROMPT_BLOCKS) * BLK

    def one_rollout(package):
        query, fresh_kv, past_kv, length, prompt = package
        start = (SYS_BLOCKS + prompt * PROMPT_BLOCKS).astype(jnp.int32)
        chosen = jnp.concatenate([slot_of[:SYS_BLOCKS], lax.dynamic_slice_in_dim(slot_of, start, PROMPT_BLOCKS, 0)])
        shared = prefix_key_value_pool[:, chosen].reshape(2, prefix_count, KV_HEADS, HEAD_SIZE)
        all_keys = jnp.concatenate([shared[0], past_kv[0].reshape(RMAX, KV_HEADS, HEAD_SIZE), fresh_kv[0].reshape(NEW, KV_HEADS, HEAD_SIZE)], 0)
        all_values = jnp.concatenate([shared[1], past_kv[1].reshape(RMAX, KV_HEADS, HEAD_SIZE), fresh_kv[1].reshape(NEW, KV_HEADS, HEAD_SIZE)], 0)
        past_positions = jnp.arange(RMAX, dtype=jnp.int32)
        new_positions = jnp.arange(NEW, dtype=jnp.int32)
        visible = jnp.concatenate([jnp.ones((NEW, prefix_count), bool), jnp.broadcast_to(past_positions[None, :] < length, (NEW, RMAX)), new_positions[None, :] <= new_positions[:, None]], 1)
        grouped = query.reshape(NEW, KV_HEADS, per_group, HEAD_SIZE).astype(jnp.float32)
        scores = jnp.einsum('ngqh,tgh->ngqt', grouped, all_keys.astype(jnp.float32)) * SCALE
        capped = SOFTCAP * jnp.tanh(scores / SOFTCAP)
        weights = jnp.where(visible[:, None, None, :], jnp.exp(capped), 0.0)
        weight_sum = lax.optimization_barrier(jnp.sum(weights, axis=-1))
        rounded = lax.optimization_barrier(weights.astype(jnp.bfloat16))
        weighted = jnp.einsum('ngqt,tgh->ngqh', rounded.astype(jnp.float32), all_values.astype(jnp.float32))
        return (weighted / weight_sum[..., None]).reshape(NEW, QUERY_HEADS * HEAD_SIZE).astype(jnp.bfloat16)
    attention_output = lax.map(one_rollout, (queries, jnp.swapaxes(incoming_key_value, 0, 1), jnp.swapaxes(response_key_value, 0, 1), lengths, rollout_task_map[:, 0]))
    attention_rows = attention_output.reshape(ROLLOUTS * NEW, QUERY_HEADS * HEAD_SIZE)
    low_rank_output = jnp.dot(attention_rows, adapter_down_weight, preferred_element_type=jnp.float32)
    adapter_output = jnp.dot(attention_rows, output_projection_weight, preferred_element_type=jnp.float32) + jnp.dot(low_rank_output, adapter_up_weight.astype(jnp.float32), precision=lax.Precision.HIGHEST)
    squares = lax.optimization_barrier(jnp.sum(adapter_output * adapter_output, axis=1)) / MODEL_WIDTH
    normed = adapter_output * lax.rsqrt(squares + EPS)[:, None] * post_norm_gain
    stream = residual.reshape(ROLLOUTS * NEW, MODEL_WIDTH).astype(jnp.float32) + normed
    power = lax.optimization_barrier(jnp.sum(stream * stream, axis=1)) / MODEL_WIDTH
    value_score = lax.optimization_barrier(jnp.sum(stream * value_head_weight, axis=1)) * lax.rsqrt(power + EPS)
    return (stream.astype(jnp.bfloat16).reshape(ROLLOUTS, NEW, MODEL_WIDTH), value_score.reshape(ROLLOUTS, NEW))
```

```python
import functools

import jax
import jax.numpy as jnp
from jax import lax
from jax.experimental import pallas as pl
from jax.experimental.pallas import tpu as pltpu
from jax.sharding import PartitionSpec as P

MODEL_WIDTH = 4608
HEAD = 128
PROMPT_BLOCKS = 16
EPS = 1e-06
C1 = 144.0 ** (-0.5) / 50.0
C2 = 50.0 * 1.4426950408889634

NY, NZ, NH = 4, 8, 8
ROWS = 64
WIDTH = 512
HEADS = 4
CHUNK = 576
PADDED = 640
MIB = 1 << 20
MESH = pl.DeviceIdType.MESH
F32 = jnp.float32
BF16 = jnp.bfloat16


def weight_of(scores):
    return jnp.exp2(jnp.tanh(scores * C1) * C2)


def dot_t(a, b):
    return lax.dot_general(a, b, (((1,), (1,)), ((), ())), preferred_element_type=F32)


def dot(a, b):
    return jnp.dot(a, b, preferred_element_type=F32)


def lane_sum(p):
    total = p[:, :HEAD]
    for i in range(1, p.shape[1] // HEAD):
        total = total + p[:, i * HEAD : (i + 1) * HEAD]
    return total


def position():
    seq = lax.axis_index("seq")
    head = lax.axis_index("head")
    return lax.div(seq, NZ), lax.rem(seq, NZ), head


def wrap(v, n):
    return lax.rem(v + 2 * n, n)


def shifted(y, z, head, axis, step):
    if axis == 0:
        return (wrap(y + step, NY) * NZ + z, head)
    return (y * NZ + wrap(z + step, NZ), head)


def cols(h):
    return slice(h * HEAD, (h + 1) * HEAD)


def gather_kernel(
    len_ref, q_ref, inc_ref, resp_ref, qall, oloc, lloc, cache, load_sem, s1, r1, s2, r2
):
    y, z, head = position()
    loads = []
    for i in range(4):
        c = pltpu.make_async_copy(resp_ref.at[:, i], cache.at[i], load_sem.at[i])
        c.start()
        loads.append(c)

    barrier = pltpu.get_barrier_semaphore()
    for axis in (0, 1):
        for step in (1, -1):
            pl.semaphore_signal(
                barrier, inc=1, device_id=shifted(y, z, head, axis, step), device_id_type=MESH
            )
    qall[y, z] = q_ref[...]
    pl.semaphore_wait(barrier, 4)

    def attend(i):
        loads[i].wait()
        length = len_ref[i]
        rows = slice(i * 16, (i + 1) * 16)
        for g in range(2):
            lhs = jnp.concatenate([q_ref[rows, cols(2 * g)], q_ref[rows, cols(2 * g + 1)]], axis=0)
            out = jnp.zeros((32, HEAD), F32)
            total = jnp.zeros((32, HEAD), F32)
            for part in range(4):
                at = slice(part * 512, (part + 1) * 512)
                p = weight_of(dot_t(lhs, cache[i, 0, at, cols(g)]))
                where = lax.broadcasted_iota(jnp.int32, p.shape, 1) + part * 512
                p = jnp.where(where < length, p, 0.0)
                total = total + lane_sum(p)
                out = out + dot(p.astype(BF16), cache[i, 1, at, cols(g)])
            p = weight_of(dot_t(lhs, inc_ref[0, i, :, cols(g)]))
            n = lax.rem(lax.broadcasted_iota(jnp.int32, p.shape, 0), 16)
            m = lax.broadcasted_iota(jnp.int32, p.shape, 1)
            p = jnp.where(m <= n, p, 0.0)
            out = out + dot(p.astype(BF16), inc_ref[1, i, :, cols(g)])
            sums = jnp.sum(total, axis=1, keepdims=True) + jnp.sum(p, axis=1, keepdims=True)
            wide = jnp.broadcast_to(sums, (32, HEAD))
            for j in range(2):
                oloc[rows, cols(2 * g + j)] = out[j * 16 : (j + 1) * 16]
                lloc[rows, cols(2 * g + j)] = wide[j * 16 : (j + 1) * 16]

    def run(axis1):
        axis2 = 1 - axis1
        n1, n2 = (NY, NZ) if axis1 == 0 else (NZ, NY)
        c1, c2 = (y, z) if axis1 == 0 else (z, y)
        h1, h2 = n1 // 2, n2 // 2

        def piece(i1, i2, part):
            a, b = (i1, i2) if axis1 == 0 else (i2, i1)
            view = qall.at[a, b]
            if part is None:
                return view
            return view.at[pl.ds(part * (ROWS // 2), ROWS // 2)]

        def first(d, k):
            s = 1 - 2 * d
            view = piece(wrap(c1 - s * k, n1), c2, d if k == h1 - 1 else None)
            return pltpu.make_async_remote_copy(
                src_ref=view,
                dst_ref=view,
                send_sem=s1.at[d, k],
                recv_sem=r1.at[d, k],
                device_id=shifted(y, z, head, axis1, s),
                device_id_type=MESH,
            )

        offsets = [0]
        for k in range(1, h1):
            offsets += [-k, k]
        offsets.append(h1)

        def second(j, d, k):
            s = 1 - 2 * d
            view = piece(wrap(c1 + offsets[j], n1), wrap(c2 - s * k, n2), d if k == h2 - 1 else None)
            return pltpu.make_async_remote_copy(
                src_ref=view,
                dst_ref=view,
                send_sem=s2.at[d, j, k],
                recv_sem=r2.at[d, j, k],
                device_id=shifted(y, z, head, axis2, s),
                device_id_type=MESH,
            )

        pending = list(range(4))
        sent = []

        def go(copy):
            copy.start()
            sent.append(copy)

        for d in (0, 1):
            go(first(d, 0))
        for d in (0, 1):
            go(second(0, d, 0))
        for k in range(h1):
            if pending and k < 1:
                attend(pending.pop(0))
            for d in (0, 1):
                first(d, k).wait_recv()
                if k < h1 - 1:
                    go(first(d, k + 1))
            if k < h1 - 1:
                for d in (0, 1):
                    j = 1 + 2 * k + d
                    for e in (0, 1):
                        go(second(j, e, 0))
            else:
                for e in (0, 1):
                    go(second(n1 - 1, e, 0))
        for k in range(h2):
            for j in range(n1):
                if pending and j % 2 == 1:
                    attend(pending.pop(0))
                for d in (0, 1):
                    second(j, d, k).wait_recv()
                    if k < h2 - 1:
                        go(second(j, d, k + 1))
        for i in pending:
            attend(i)
        for copy in sent:
            copy.wait_send()

    core = lax.rem(head, 2)

    @pl.when(core == 0)
    def _():
        run(0)

    @pl.when(core == 1)
    def _():
        run(1)


def prefix_kernel(rc, map_ref, slot_ref, q_ref, pool_ref, o_ref, l_ref, acc, lanes, sbuf, qbuf, obuf, lbuf, lists, counts, system, meta):
    prompts = counts.shape[0]
    capacity = lists.shape[1]
    rollouts = map_ref.shape[0]
    slots = slot_ref.shape[0]
    sys_blocks = meta
    total_rows = q_ref.shape[0]
    chunks = total_rows // rc

    def note(i, n):
        is_sys = slot_ref[i] < sys_blocks

        @pl.when(is_sys)
        def _():
            system[n] = i

        return n + is_sys.astype(jnp.int32)

    count = lax.fori_loop(0, slots, note, 0)

    def clear(i, _):
        counts[i] = 0
        return 0

    lax.fori_loop(0, prompts, clear, 0)

    def member(r, _):
        p = map_ref[r]
        n = counts[p]
        lists[p, n] = r
        counts[p] = n + 1
        return 0

    lax.fori_loop(0, rollouts, member, 0)

    def rows_of(c):
        return pl.ds(pl.multiple_of(c * rc, rc), rc)

    def score(item, h):
        c = lax.div(item, count)
        b = system[lax.rem(item, count)]
        return dot_t(q_ref[rows_of(c), cols(h)], pool_ref[0, b, :, cols(h // 2)])

    @pl.when(count == 0)
    def _():
        acc[...] = jnp.zeros_like(acc)
        lanes[...] = jnp.zeros_like(lanes)

    @pl.when(count > 0)
    def _():
        items = count * chunks
        sbuf[0] = score(0, 0)

        def step(item, _):
            rows = rows_of(lax.div(item, count))
            turn = lax.rem(item, count)
            b = system[turn]
            first = turn == 0
            following = jnp.minimum(item + 1, items - 1)
            for h in range(HEADS):
                if h < HEADS - 1:
                    sbuf[(h + 1) % 2] = score(item, h + 1)
                else:
                    sbuf[0] = score(following, 0)
                p = weight_of(sbuf[h % 2])
                part = lane_sum(p)
                out = dot(p.astype(BF16), pool_ref[1, b, :, cols(h // 2)])
                lanes[rows, cols(h)] = jnp.where(first, 0.0, lanes[rows, cols(h)]) + part
                acc[rows, cols(h)] = jnp.where(first, 0.0, acc[rows, cols(h)]) + out
            return 0

        lax.fori_loop(0, items, step, 0)

    def prompt_slot(i, _):
        logical = slot_ref[i]

        @pl.when(logical >= sys_blocks)
        def _():
            p = lax.div(logical - sys_blocks, PROMPT_BLOCKS)
            n = counts[p]

            def pick(m, _):
                r = lists[p, m]
                qbuf[pl.ds(pl.multiple_of(m * 16, 16), 16), :] = q_ref[
                    pl.ds(pl.multiple_of(r * 16, 16), 16), :
                ]
                return 0

            lax.fori_loop(0, n, pick, 0)

            def part(c, _):
                rows = pl.ds(pl.multiple_of(c * 128, 128), 128)
                for h in range(HEADS):
                    w = weight_of(dot_t(qbuf[rows, cols(h)], pool_ref[0, i, :, cols(h // 2)]))
                    lbuf[rows, cols(h)] = lane_sum(w)
                    obuf[rows, cols(h)] = dot(w.astype(BF16), pool_ref[1, i, :, cols(h // 2)])
                return 0

            lax.fori_loop(0, lax.div(n + 7, 8), part, 0)

            def put(m, _):
                r = lists[p, m]
                at = pl.ds(pl.multiple_of(r * 16, 16), 16)
                src = pl.ds(pl.multiple_of(m * 16, 16), 16)
                acc[at, :] += obuf[src, :]
                lanes[at, :] += lbuf[src, :]
                return 0

            lax.fori_loop(0, n, put, 0)

        return 0

    lax.fori_loop(0, slots, prompt_slot, 0)

    lane = lax.broadcasted_iota(jnp.int32, (8, WIDTH), 1)
    row = lax.broadcasted_iota(jnp.int32, (8, WIDTH), 0)
    pick_head = jnp.where(lax.div(lane, HEAD) == row, 1.0, 0.0).astype(BF16)

    def finish(d, _):
        at = pl.ds(pl.multiple_of(d * ROWS, ROWS), ROWS)
        o_ref[at, :] = acc[at, :].astype(BF16)
        v = lanes[at, :]
        hi = v.astype(BF16)
        lo = (v - hi.astype(F32)).astype(BF16)
        l_ref[d] = jnp.zeros((8, HEAD), F32)
        l_ref[d, :, :ROWS] = dot_t(pick_head, hi) + dot_t(pick_head, lo)
        return 0

    lax.fori_loop(0, total_rows // ROWS, finish, 0)


def finish_kernel(
    o_ref, l_ref, oloc, lloc, res_ref, w_ref, down_ref, up_ref, gain_ref, vhw_ref,
    hid_ref, val_ref,
    wbuf, part1, lpart1, mine, pmine, rbuf, rlbuf, rbuf2, rlbuf2, chunk, rchunk, small, rsmall,
    w_sem, s1, r1, t1, u1, s2, r2, t2, u2, hs, hr, ss, sr,
):
    y, z, head = position()
    wcopy = pltpu.make_async_copy(w_ref, wbuf, w_sem)
    wcopy.start()

    barrier = pltpu.get_barrier_semaphore()
    for axis in (0, 1):
        for step in (1, -1):
            pl.semaphore_signal(
                barrier, inc=1, device_id=shifted(y, z, head, axis, step), device_id_type=MESH
            )
    seq = y * NZ + z
    for t in range(1, NH):
        pl.semaphore_signal(
            barrier, inc=1, device_id=(seq, wrap(head + t, NH)), device_id_type=MESH
        )
    pl.semaphore_wait(barrier, 4 + NH - 1)

    half = ROWS // 2

    def reduce(axis, n, c, pieces, own, own_l, rb, rl, ss_, rs_, ts_, us_, final, final_l):
        h = n // 2
        sent = []

        def side(view, d):
            return view.at[pl.ds(d * half, half)]

        def copy(d, k, j):
            s = 1 - 2 * d
            if k == 0:
                src = side(own(wrap(c + s * h, n), j), d)
                dst = side(rb.at[d, 0, j], d)
            else:
                src = rb.at[d, k - 1, j]
                dst = rb.at[d, k, j]
            return pltpu.make_async_remote_copy(
                src_ref=src, dst_ref=dst, send_sem=ss_.at[d, k, j], recv_sem=rs_.at[d, k, j],
                device_id=shifted(y, z, head, axis, s), device_id_type=MESH,
            )

        def copy_l(d, k):
            s = 1 - 2 * d
            src = own_l(wrap(c + s * (h if d == 0 else h - 1), n)) if k == 0 else rl.at[d, k - 1]
            return pltpu.make_async_remote_copy(
                src_ref=src, dst_ref=rl.at[d, k], send_sem=ts_.at[d, k], recv_sem=us_.at[d, k],
                device_id=shifted(y, z, head, axis, s), device_id_type=MESH,
            )

        def go(x):
            x.start()
            sent.append(x)

        steps_l = (h, h - 1)
        for j in range(pieces):
            for d in (0, 1):
                go(copy(d, 0, j))
            if j == 0:
                for d in (0, 1):
                    go(copy_l(d, 0))
        for k in range(1, h):
            for j in range(pieces):
                for d in (0, 1):
                    s = 1 - 2 * d
                    copy(d, k - 1, j).wait_recv()
                    mine_here = own(wrap(c + s * (h - k), n), j)
                    if k == 1:
                        a = pl.ds(d * half, half)
                        b = pl.ds((1 - d) * half, half)
                        rb[d, 0, j, a] = (rb[d, 0, j, a].astype(F32) + mine_here[a].astype(F32)).astype(BF16)
                        rb[d, 0, j, b] = mine_here[b]
                    else:
                        rb[d, k - 1, j] = (rb[d, k - 1, j].astype(F32) + mine_here[...].astype(F32)).astype(BF16)
                    go(copy(d, k, j))
                if j == 0:
                    for d in (0, 1):
                        if k < steps_l[d]:
                            s = 1 - 2 * d
                            copy_l(d, k - 1).wait_recv()
                            rl[d, k - 1] = rl[d, k - 1] + own_l(wrap(c + s * (steps_l[d] - k), n))[...]
                            go(copy_l(d, k))
        for j in range(pieces):
            for d in (0, 1):
                copy(d, h - 1, j).wait_recv()
            final(j, own(c, j)[...].astype(F32) + rb[0, h - 1, j].astype(F32) + rb[1, h - 1, j].astype(F32))
            if j == 0:
                for d in (0, 1):
                    copy_l(d, steps_l[d] - 1).wait_recv()
                final_l(own_l(c)[...] + rl[0, steps_l[0] - 1] + rl[1, steps_l[1] - 1])
        for x in sent:
            x.wait_send()

    def run(axis1):
        axis2 = 1 - axis1
        n1, n2 = (NY, NZ) if axis1 == 0 else (NZ, NY)
        c1, c2 = (y, z) if axis1 == 0 else (z, y)

        def own(i, j):
            return o_ref.at[i, j] if axis1 == 0 else o_ref.at[j, i]

        def own_l(i):
            return l_ref.at[i] if axis1 == 0 else l_ref.at[:, i]

        def keep(j, v):
            part1[j] = v.astype(BF16)

            @pl.when(c2 == j)
            def _():
                mine[...] = v

        def keep_l(v):
            lpart1[pl.ds(0, n2)] = v

        reduce(
            axis1, n1, c1, n2, own, own_l,
            rbuf_view(n1, n2),
            rlbuf_view(n1, n2), s1, r1, t1, u1, keep, keep_l,
        )

        def own2(i, j):
            return part1.at[i]

        def own2_l(i):
            return lpart1.at[i]

        def keep2(j, v):
            mine[...] = v - part1[c2].astype(F32) + mine[...]

        def keep2_l(v):
            small[...] = v

        reduce(axis2, n2, c2, 1, own2, own2_l, rbuf2, rlbuf2, s2, r2, t2, u2, keep2, keep2_l)

    def rbuf_view(n1, n2):
        return rbuf[0] if n1 == NY else rbuf[1]

    def rlbuf_view(n1, n2):
        return rlbuf[0] if n1 == NY else rlbuf[1]

    core = lax.rem(head, 2)

    @pl.when(core == 0)
    def _():
        run(1)

    @pl.when(core == 1)
    def _():
        run(0)

    sums = jnp.transpose(jnp.concatenate([small[...], jnp.zeros((HEAD - 8, HEAD), F32)], axis=0))
    att = []
    for h in range(HEADS):
        den = sums[:ROWS, h : h + 1] + lloc[:, cols(h)]
        att.append(((mine[:, cols(h)] + oloc[:, cols(h)]) / den).astype(BF16))
    att = jnp.concatenate(att, axis=1)
    low = dot(att, down_ref[...])
    low_hi = low.astype(BF16)
    low_lo = (low - low_hi.astype(F32)).astype(BF16)
    low_lo2 = (low - low_hi.astype(F32) - low_lo.astype(F32)).astype(BF16)
    wcopy.wait()
    for j in range(NH):
        a = (j * CHUNK) // HEAD * HEAD
        b = a + PADDED
        v = dot(att, wbuf[:, a:b])
        u = up_ref[:, a:b]
        v = v + (dot(low_hi, u) + dot(low_lo, u) + dot(low_lo2, u))
        chunk[j] = v[:, j * CHUNK - a : j * CHUNK - a + CHUNK].astype(BF16)

        @pl.when(head == j)
        def _():
            pmine[...] = v[:, j * CHUNK - a : j * CHUNK - a + CHUNK]

    sends = []
    for t in range(1, NH):
        to = wrap(head + t, NH)
        x = pltpu.make_async_remote_copy(
            src_ref=chunk.at[to], dst_ref=rchunk.at[t - 1], send_sem=hs.at[t - 1], recv_sem=hr.at[t - 1],
            device_id=(seq, to), device_id_type=MESH,
        )
        x.start()
        sends.append(x)
    p = pmine[...]
    for t in range(1, NH):
        sends[t - 1].wait_recv()
        p = p + rchunk[t - 1].astype(F32)

    res = res_ref[...].astype(F32)
    gain = gain_ref[...]
    vhw = vhw_ref[...]
    pg = p * gain
    parts = [p * p, res * res, res * pg, pg * pg, res * vhw, pg * vhw]
    lane = lax.broadcasted_iota(jnp.int32, (ROWS, HEAD), 1)
    packed = jnp.zeros((ROWS, HEAD), F32)
    for i, v in enumerate(parts):
        packed = jnp.where(lane == i, jnp.sum(v, axis=1, keepdims=True), packed)
    packed = jnp.concatenate([packed, jnp.zeros((HEAD - ROWS, HEAD), F32)], axis=0)
    small[...] = jnp.transpose(packed)[:8]
    sends2 = []
    for t in range(1, NH):
        x = pltpu.make_async_remote_copy(
            src_ref=small, dst_ref=rsmall.at[t - 1], send_sem=ss.at[t - 1], recv_sem=sr.at[t - 1],
            device_id=(seq, wrap(head + t, NH)), device_id_type=MESH,
        )
        x.start()
        sends2.append(x)
    total = small[...]
    for t in range(1, NH):
        sends2[t - 1].wait_recv()
        total = total + rsmall[t - 1]
    sq, res2, rpg, pg2, rw, pgw = [total[i : i + 1] for i in range(6)]
    r = lax.rsqrt(sq / MODEL_WIDTH + EPS)
    power = res2 + 2.0 * r * rpg + r * r * pg2
    value = (rw + r * pgw) * lax.rsqrt(power / MODEL_WIDTH + EPS)
    for i in range(4):
        val_ref[i : i + 1, :] = value[:, i * 16 : (i + 1) * 16]
    rcol = jnp.transpose(jnp.broadcast_to(r, (HEAD, HEAD)))[:ROWS, :1]
    hid_ref[...] = (res + pg * rcol).astype(BF16)
    for x in sends + sends2:
        x.wait_send()


def finish_entry(*refs):
    refs = list(refs)
    ins, outs = refs[:10], refs[10:12]
    s = refs[12:]
    wbuf, part1, lpart1, mine, pmine, rb_y, rb_z, rl_y, rl_z = s[:9]
    finish_kernel(
        *ins, *outs, wbuf, part1, lpart1, mine, pmine, (rb_y, rb_z), (rl_y, rl_z), *s[9:]
    )


def local(
    queries, incoming_key_value, prefix_key_value_pool, response_key_value, residual, lengths,
    rollout_task_map, slot_block_table, output_projection_weight, adapter_down_weight,
    adapter_up_weight, post_norm_gain, value_head_weight,
):
    vmem = pl.BlockSpec(memory_space=pltpu.VMEM)
    smem = pl.BlockSpec(memory_space=pltpu.SMEM)
    anyw = pl.BlockSpec(memory_space=pl.ANY)
    dma = pltpu.SemaphoreType.DMA
    sds = jax.ShapeDtypeStruct
    devices = NY * NZ
    rows_all = devices * ROWS

    qall, oloc, lloc = pl.pallas_call(
        gather_kernel,
        out_shape=(
            sds((NY, NZ, ROWS, WIDTH), BF16),
            sds((ROWS, WIDTH), F32),
            sds((ROWS, WIDTH), F32),
        ),
        in_specs=[smem, vmem, vmem, anyw],
        out_specs=(vmem, vmem, vmem),
        scratch_shapes=[
            pltpu.VMEM((4, 2, 2048, 256), BF16),
            dma((4,)),
            dma((2, NZ // 2)),
            dma((2, NZ // 2)),
            dma((2, NZ, NZ // 2)),
            dma((2, NZ, NZ // 2)),
        ],
        compiler_params=pltpu.CompilerParams(
            collective_id=0, has_side_effects=True, vmem_limit_bytes=40 * MIB
        ),
        name="gather_queries",
    )(lengths, queries.reshape(ROWS, WIDTH), incoming_key_value, response_key_value)

    rc = 1024
    prompts = 12
    o, l = pl.pallas_call(
        functools.partial(prefix_kernel_entry, rc),
        out_shape=(sds((rows_all, WIDTH), BF16), sds((devices, 8, HEAD), F32)),
        in_specs=[smem, smem, vmem, vmem],
        out_specs=(vmem, vmem),
        scratch_shapes=[
            pltpu.VMEM((rows_all, WIDTH), F32),
            pltpu.VMEM((rows_all, WIDTH), F32),
            pltpu.VMEM((2, rc, 512), F32),
            pltpu.VMEM((384, WIDTH), BF16),
            pltpu.VMEM((384, WIDTH), F32),
            pltpu.VMEM((384, WIDTH), F32),
            pltpu.SMEM((prompts, 128), jnp.int32),
            pltpu.SMEM((prompts,), jnp.int32),
            pltpu.SMEM((8,), jnp.int32),
        ],
        compiler_params=pltpu.CompilerParams(vmem_limit_bytes=56 * MIB),
        name="prefix_attention",
    )(rollout_task_map.reshape(-1), slot_block_table, qall.reshape(rows_all, WIDTH), prefix_key_value_pool)

    hidden, values = pl.pallas_call(
        finish_entry,
        out_shape=(sds((ROWS, CHUNK), BF16), sds((4, 16), F32)),
        in_specs=[vmem, vmem, vmem, vmem, vmem, anyw, vmem, vmem, vmem, vmem],
        out_specs=(vmem, vmem),
        scratch_shapes=[
            pltpu.VMEM((WIDTH, MODEL_WIDTH), BF16),
            pltpu.VMEM((NZ, ROWS, WIDTH), BF16),
            pltpu.VMEM((NZ, 8, HEAD), F32),
            pltpu.VMEM((ROWS, WIDTH), F32),
            pltpu.VMEM((ROWS, CHUNK), F32),
            pltpu.VMEM((2, NY // 2, NZ, ROWS, WIDTH), BF16),
            pltpu.VMEM((2, NZ // 2, NY, ROWS, WIDTH), BF16),
            pltpu.VMEM((2, NY // 2, NZ, 8, HEAD), F32),
            pltpu.VMEM((2, NZ // 2, NY, 8, HEAD), F32),
            pltpu.VMEM((2, NZ // 2, 1, ROWS, WIDTH), BF16),
            pltpu.VMEM((2, NZ // 2, 8, HEAD), F32),
            pltpu.VMEM((NH, ROWS, CHUNK), BF16),
            pltpu.VMEM((NH - 1, ROWS, CHUNK), BF16),
            pltpu.VMEM((8, HEAD), F32),
            pltpu.VMEM((NH - 1, 8, HEAD), F32),
            dma(()),
            dma((2, NZ // 2, NZ)),
            dma((2, NZ // 2, NZ)),
            dma((2, NZ // 2)),
            dma((2, NZ // 2)),
            dma((2, NZ // 2, 1)),
            dma((2, NZ // 2, 1)),
            dma((2, NZ // 2)),
            dma((2, NZ // 2)),
            dma((NH - 1,)),
            dma((NH - 1,)),
            dma((NH - 1,)),
            dma((NH - 1,)),
        ],
        compiler_params=pltpu.CompilerParams(
            collective_id=1, has_side_effects=True, vmem_limit_bytes=48 * MIB
        ),
        name="reduce_and_project",
    )(
        o.reshape(NY, NZ, ROWS, WIDTH), l.reshape(NY, NZ, 8, HEAD), oloc, lloc,
        residual.reshape(ROWS, CHUNK), output_projection_weight, adapter_down_weight,
        adapter_up_weight, post_norm_gain.reshape(1, CHUNK), value_head_weight.reshape(1, CHUNK),
    )
    return hidden.reshape(residual.shape), values


def prefix_kernel_entry(rc, *refs):
    prefix_kernel(rc, *refs, 64)


def solution(mesh):
    placed = (
        P("seq", None, "head"),
        P(None, "seq", None, "head"),
        P(None, "seq", None, "head"),
        P(None, "seq", None, "head"),
        P("seq", None, "head"),
        P("seq"),
        P(),
        P("seq"),
        P("head", None),
        P("head", None),
        P(),
        P("head"),
        P("head"),
    )
    return jax.shard_map(
        local,
        mesh=mesh,
        in_specs=placed,
        out_specs=(P("seq", None, "head"), P("seq", None)),
        check_vma=False,
    )
```

```python
import functools

import jax
import jax.numpy as jnp
from jax import lax
from jax.experimental import pallas as pl
from jax.experimental.pallas import tpu as pltpu
from jax.sharding import PartitionSpec as P

MODEL_WIDTH = 4608
HEAD = 128
SYS_BLOCKS = 64
PROMPT_BLOCKS = 16
EPS = 1e-06
C1 = 144.0 ** (-0.5) / 50.0
C2 = 50.0 * 1.4426950408889634

NY, NZ, NH = 4, 8, 8
ROWS = 64
WIDTH = 512
HEADS = 4
CHUNK = 576
GROUP = 12
PADDED = 640
MIB = 1 << 20
K1_MIB, K2_MIB, K3_MIB = 58, 58, 58
MESH = pl.DeviceIdType.MESH
F32 = jnp.float32
BF16 = jnp.bfloat16


def weight_of(scores):
    return jnp.exp2(jnp.tanh(scores * C1) * C2)


def dot_t(a, b):
    return lax.dot_general(a, b, (((1,), (1,)), ((), ())), preferred_element_type=F32)


def dot(a, b):
    return jnp.dot(a, b, preferred_element_type=F32)


def lane_sum(p):
    total = p[:, :HEAD]
    for i in range(1, p.shape[1] // HEAD):
        total = total + p[:, i * HEAD : (i + 1) * HEAD]
    return total


def position():
    seq = lax.axis_index("seq")
    head = lax.axis_index("head")
    return lax.div(seq, NZ), lax.rem(seq, NZ), head


def wrap(v, n):
    return lax.rem(v + 2 * n, n)


def shifted(y, z, head, axis, step):
    if axis == 0:
        return (wrap(y + step, NY) * NZ + z, head)
    return (y * NZ + wrap(z + step, NZ), head)


def cols(h):
    return slice(h * HEAD, (h + 1) * HEAD)


def chosen(slot_ref, sys_blocks, ranks):
    found = [jnp.int32(0) for _ in ranks]
    seen = jnp.int32(0)
    for i in range(slot_ref.shape[0]):
        is_sys = (slot_ref[i] < sys_blocks).astype(jnp.int32)
        for n, rank in enumerate(ranks):
            found[n] = found[n] + i * is_sys * (seen == rank).astype(jnp.int32)
        seen = seen + is_sys
    return [(f, jnp.where(seen > rank, 1.0, 0.0)) for f, rank in zip(found, ranks)]


def head_picker():
    lane = lax.broadcasted_iota(jnp.int32, (8, WIDTH), 1)
    row = lax.broadcasted_iota(jnp.int32, (8, WIDTH), 0)
    return jnp.where(lax.div(lane, HEAD) == row, 1.0, 0.0).astype(BF16)


def head_sums(picker, lanes):
    hi = lanes.astype(BF16)
    lo = (lanes - hi.astype(F32)).astype(BF16)
    return dot_t(picker, hi) + dot_t(picker, lo)


def system_round(load_q, store, pool, picks, qtmp, sbuf, otmp, lbuf, arrived=None):
    for m in range(8):
        qtmp[m * ROWS : (m + 1) * ROWS, :] = load_q(m)
    (b0, v0), (b1, v1) = picks

    def score(h, b):
        return dot_t(qtmp[:, cols(h)], pool[0, b, :, cols(h // 2)])

    sbuf[0] = score(0, b0)
    for h in range(HEADS):
        g = h // 2
        sbuf[1] = score(h, b1)
        p0 = weight_of(sbuf[0])
        l0 = lane_sum(p0)
        o0 = dot(p0.astype(BF16), pool[1, b0, :, cols(g)])
        if h < HEADS - 1:
            sbuf[0] = score(h + 1, b0)
        p1 = weight_of(sbuf[1])
        l1 = lane_sum(p1)
        o1 = dot(p1.astype(BF16), pool[1, b1, :, cols(g)])
        otmp[:, cols(h)] = o0 * v0 + o1 * v1
        lbuf[:, cols(h)] = l0 * v0 + l1 * v1
    total = head_sums(head_picker(), lbuf[...])
    if arrived is not None:
        arrived()
    for m in range(8):
        at = slice(m * ROWS, (m + 1) * ROWS)
        store(m, otmp[at, :], total[:, at])


def gather_kernel(
    len_ref, slot_ref, q_ref, inc_ref, map_ref, resp_ref, pool_ref,
    qall, acc_out, sums, oloc, lloc, table,
    cache, pool, acc, qtmp, sbuf, otmp, lbuf, load_sem, pool_sem, acc_sem, s1, r1, s2, r2,
):
    y, z, head = position()
    core = lax.rem(head, 2)

    barrier = pltpu.get_barrier_semaphore()
    for axis in (0, 1):
        for step in (1, -1):
            pl.semaphore_signal(
                barrier, inc=1, device_id=shifted(y, z, head, axis, step), device_id_type=MESH
            )
    loads = []
    for i in range(4):
        c = pltpu.make_async_copy(resp_ref.at[:, i], cache.at[i], load_sem.at[i])
        c.start()
        loads.append(c)
    pool_load = pltpu.make_async_copy(pool_ref, pool, pool_sem)
    pool_load.start()
    qall[y, z] = q_ref[...]
    picks = chosen(slot_ref, SYS_BLOCKS, (0, 1))
    pl.semaphore_wait(barrier, 4)

    def list_members():
        task = jnp.broadcast_to(map_ref[...].astype(F32), (HEAD, HEAD))
        across = jnp.transpose(task)
        row = lax.broadcasted_iota(jnp.int32, (HEAD, HEAD), 0)
        lane = lax.broadcasted_iota(jnp.int32, (HEAD, HEAD), 1)
        earlier = jnp.where((task == across) & (lane < row), 1.0, 0.0)
        rank = jnp.sum(earlier, axis=1, keepdims=True)
        spot = jnp.where(rank == lane.astype(F32), 1.0, 0.0).astype(BF16)
        mine = across[:16] == row[:16].astype(F32)
        ids = jnp.where(mine, lane[:16].astype(F32), 0.0).astype(BF16)
        count = jnp.sum(jnp.where(mine, 1.0, 0.0), axis=1, keepdims=True)
        table[...] = jnp.where(lane[:16] == HEAD - 1, count, dot(ids, spot)).astype(jnp.int32)

    def attend(i):
        loads[i].wait()
        length = len_ref[i]
        rows = slice(i * 16, (i + 1) * 16)

        def group(g, _):
            def at(j):
                return pl.ds(pl.multiple_of((2 * g + j) * HEAD, HEAD), HEAD)

            gc = pl.ds(pl.multiple_of(g * HEAD, HEAD), HEAD)
            lhs = jnp.concatenate([q_ref[rows, at(0)], q_ref[rows, at(1)]], axis=0)
            out = jnp.zeros((32, HEAD), F32)
            total = jnp.zeros((32, HEAD), F32)
            for part in range(4):
                keys = slice(part * 512, (part + 1) * 512)
                p = weight_of(dot_t(lhs, cache[i, 0, keys, gc]))
                where = lax.broadcasted_iota(jnp.int32, p.shape, 1) + part * 512
                p = jnp.where(where < length, p, 0.0)
                total = total + lane_sum(p)
                out = out + dot(p.astype(BF16), cache[i, 1, keys, gc])
            p = weight_of(dot_t(lhs, inc_ref[0, i, :, gc]))
            n = lax.rem(lax.broadcasted_iota(jnp.int32, p.shape, 0), 16)
            m = lax.broadcasted_iota(jnp.int32, p.shape, 1)
            p = jnp.where(m <= n, p, 0.0)
            out = out + dot(p.astype(BF16), inc_ref[1, i, :, gc])
            wide = jnp.broadcast_to(
                jnp.sum(total, axis=1, keepdims=True) + jnp.sum(p, axis=1, keepdims=True), (32, HEAD)
            )
            for j in range(2):
                oloc[rows, at(j)] = out[j * 16 : (j + 1) * 16]
                lloc[rows, at(j)] = wide[j * 16 : (j + 1) * 16]
            return 0

        lax.fori_loop(0, 2, group, 0)

    def copies(axis1):
        axis2 = 1 - axis1
        n1, n2 = (NY, NZ) if axis1 == 0 else (NZ, NY)
        c1, c2 = (y, z) if axis1 == 0 else (z, y)
        h1, h2 = n1 // 2, n2 // 2
        offsets = [0]
        for k in range(1, h1):
            offsets += [-k, k]
        offsets.append(h1)

        def piece(i1, i2, part):
            a, b = (i1, i2) if axis1 == 0 else (i2, i1)
            view = qall.at[a, b]
            return view if part is None else view.at[pl.ds(part * (ROWS // 2), ROWS // 2)]

        def first(d, k):
            s = 1 - 2 * d
            view = piece(wrap(c1 - s * k, n1), c2, d if k == h1 - 1 else None)
            return pltpu.make_async_remote_copy(
                src_ref=view, dst_ref=view, send_sem=s1.at[d, k], recv_sem=r1.at[d, k],
                device_id=shifted(y, z, head, axis1, s), device_id_type=MESH,
            )

        def second(j, d, k):
            s = 1 - 2 * d
            view = piece(wrap(c1 + offsets[j], n1), wrap(c2 - s * k, n2), d if k == h2 - 1 else None)
            return pltpu.make_async_remote_copy(
                src_ref=view, dst_ref=view, send_sem=s2.at[d, j, k], recv_sem=r2.at[d, j, k],
                device_id=shifted(y, z, head, axis2, s), device_id_type=MESH,
            )

        def phase1(work):
            for d in (0, 1):
                first(d, 0).start()
            for d in (0, 1):
                second(0, d, 0).start()
            for k in range(h1):
                for i in work[k]:
                    attend(i)
                for d in (0, 1):
                    first(d, k).wait_recv()
                    if k < h1 - 1:
                        first(d, k + 1).start()
                if k < h1 - 1:
                    for d in (0, 1):
                        for e in (0, 1):
                            second(1 + 2 * k + d, e, 0).start()
                else:
                    for e in (0, 1):
                        second(n1 - 1, e, 0).start()

        def forward(k):
            for j in range(n1):
                for d in (0, 1):
                    second(j, d, k).wait_recv()
                    if k < h2 - 1:
                        second(j, d, k + 1).start()

        def drain():
            for k in range(h1):
                for d in (0, 1):
                    first(d, k).wait_send()
            for k in range(h2):
                for j in range(n1):
                    for d in (0, 1):
                        second(j, d, k).wait_send()

        return phase1, forward, drain

    def on(core_index, action):
        @pl.when(core == core_index)
        def _():
            action()

    def start0():
        phase1, forward, _ = copies(0)
        phase1(([0], [1]))
        attend(2)
        attend(3)
        list_members()
        forward(0)

    def start1():
        copies(1)[0](([0], [1], [2], [3]))
        list_members()

    on(0, start0)
    on(1, start1)
    pool_load.wait()

    def keep(at):
        return pltpu.make_async_copy(acc.at[at], acc_out.at[at], acc_sem.at[at])

    def compute(pair, y_step):
        def coords(m):
            a = wrap(z + pair[m // 4], NZ)
            return (
                jnp.where(core == 0, m % 4, wrap(y + y_step, NY)),
                jnp.where(core == 0, a, m),
            )

        def load_q(m):
            return qall[coords(m)]

        def store(m, out, total):
            at = coords(m)
            acc[at] = out
            keep(at).start()
            sums[at] = jnp.concatenate([total, jnp.zeros((8, HEAD - ROWS), F32)], axis=1)

        system_round(load_q, store, pool, picks, qtmp, sbuf, otmp, lbuf)

    def in_round(r, index, core_index, action):
        @pl.when((r == index) & (core == core_index))
        def _():
            action()

    def one_round(r, _):
        compute((r, -1 - r), jnp.where(r == 1, -1, jnp.where(r == 2, 1, jnp.where(r == 3, 2, 0))))
        for k in range(3):
            in_round(r, k, 0, lambda: copies(0)[1](k + 1))
        in_round(r, 0, 1, lambda: copies(1)[1](0))
        in_round(r, 2, 1, lambda: copies(1)[1](1))
        return 0

    lax.fori_loop(0, 4, one_round, 0)
    on(0, lambda: copies(0)[2]())
    on(1, lambda: copies(1)[2]())
    for a in range(NY):
        for b in range(NZ):
            keep((a, b)).wait()


def prefix_kernel(
    rc, slot_ref, table_ref, q_ref, pool_hbm, lin_ref, acc_out, l_ref, sel,
    pool_ref, acc, lanes, sbuf, qbuf, obuf, lbuf, system, item_slot, item_prompt, item_part, pool_sem, acc_sem,
):
    pool_load = pltpu.make_async_copy(pool_hbm, pool_ref, pool_sem)
    pool_load.start()
    slots = slot_ref.shape[0]
    total_rows = q_ref.shape[0]
    chunks = total_rows // rc

    for i in range(8):
        system[i] = 0
    count = jnp.int32(0)
    items_p = jnp.int32(0)
    for i in range(slots):
        logical = slot_ref[i]
        system[count] = i
        count = count + (logical < SYS_BLOCKS).astype(jnp.int32)
        p = lax.div(jnp.maximum(logical - SYS_BLOCKS, 0), PROMPT_BLOCKS)
        n = jnp.where(logical < SYS_BLOCKS, 0, table_ref[p, HEAD - 1])
        for c in range(2):
            item_slot[items_p] = i
            item_prompt[items_p] = p
            item_part[items_p] = c
            items_p = items_p + (n > c * GROUP).astype(jnp.int32)
    count = jnp.maximum(count - 4, 0)

    def rows_of(c):
        return pl.ds(pl.multiple_of(c * rc, rc), rc)

    def score(item, h):
        c = lax.div(item, count)
        b = system[4 + lax.rem(item, count)]
        return dot_t(q_ref[rows_of(c), cols(h)], pool_ref[0, b, :, cols(h // 2)])

    acc[...] = jnp.zeros_like(acc)
    lanes[...] = jnp.zeros_like(lanes)
    pool_load.wait()
    for n in range(2):
        for kv in range(2):
            sel[kv, n] = pool_ref[kv, system[2 + n]]

    @pl.when(count > 0)
    def _():
        items = count * chunks
        sbuf[0] = score(0, 0)

        def step(item, _):
            rows = rows_of(lax.div(item, count))
            turn = lax.rem(item, count)
            b = system[4 + turn]
            following = jnp.minimum(item + 1, items - 1)
            for h in range(HEADS):
                if h < HEADS - 1:
                    sbuf[(h + 1) % 2] = score(item, h + 1)
                else:
                    sbuf[0] = score(following, 0)
                p = weight_of(sbuf[h % 2])
                part = lane_sum(p)
                out = dot(p.astype(BF16), pool_ref[1, b, :, cols(h // 2)])
                lanes[rows, cols(h)] += part
                acc[rows, cols(h)] += out
            return 0

        lax.fori_loop(0, items, step, 0)

    rows_g = GROUP * 16

    def pick(k, turn):
        p = item_prompt[k]
        c = item_part[k]
        for m in range(GROUP):
            r = table_ref[p, c * GROUP + m]
            qbuf[turn, m * 16 : (m + 1) * 16, :] = q_ref[pl.ds(pl.multiple_of(r * 16, 16), 16), :]

    def member_score(k, turn, g):
        lhs = jnp.concatenate([qbuf[turn, :, cols(2 * g)], qbuf[turn, :, cols(2 * g + 1)]], axis=0)
        return dot_t(lhs, pool_ref[0, item_slot[k], :, cols(g)])

    def member_weights(k, g):
        w = weight_of(sbuf[g, : 2 * rows_g])
        part = lane_sum(w)
        out = dot(w.astype(BF16), pool_ref[1, item_slot[k], :, cols(g)])
        for j in range(2):
            at = slice(j * rows_g, (j + 1) * rows_g)
            obuf[:, cols(2 * g + j)] = out[at]
            lbuf[:, cols(2 * g + j)] = part[at]

    @pl.when(items_p > 0)
    def _():
        pick(0, 0)
        sbuf[0, : 2 * rows_g] = member_score(0, 0, 0)

        def one(k, _):
            turn = lax.rem(k, 2)
            following = jnp.minimum(k + 1, items_p - 1)
            sbuf[1, : 2 * rows_g] = member_score(k, turn, 1)
            pick(following, 1 - turn)
            member_weights(k, 0)
            sbuf[0, : 2 * rows_g] = member_score(following, 1 - turn, 0)
            member_weights(k, 1)
            p = item_prompt[k]
            c = item_part[k]
            n = table_ref[p, HEAD - 1]
            for m in range(GROUP):
                r = table_ref[p, c * GROUP + m]
                at = pl.ds(pl.multiple_of(r * 16, 16), 16)
                src = slice(m * 16, (m + 1) * 16)
                there = jnp.where(c * GROUP + m < n, 1.0, 0.0)
                acc[at, :] += obuf[src, :] * there
                lanes[at, :] += lbuf[src, :] * there
            return 0

        lax.fori_loop(0, items_p, one, 0)

    acc_store = pltpu.make_async_copy(acc, acc_out, acc_sem)
    acc_store.start()
    picker = head_picker()

    def finish(c, _):
        total = head_sums(picker, lanes[pl.ds(pl.multiple_of(c * 512, 512), 512), :])
        for m in range(8):
            l_ref[c * 8 + m] = lin_ref[c * 8 + m]
            l_ref[c * 8 + m, :, :ROWS] += total[:, m * ROWS : (m + 1) * ROWS]
        return 0

    lax.fori_loop(0, total_rows // 512, finish, 0)
    acc_store.wait()


def finish_kernel(
    slot_ref, l_ref, q_ref, oloc, lloc, res_ref, pool, first_ref, second_ref, w_ref, down_ref, up_ref, gain_ref, vhw_ref,
    hid_ref, val_ref,
    wbuf, acc, acc2, sums, far, qtmp, sbuf, otmp, lbuf, part1, lpart1, mine, pmine,
    rb_y, rb_z, rl_y, rl_z, rb2, rl2, chunk, rchunk, small, rsmall,
    w_sem, a_sem, s1, r1, t1, u1, s2, r2, t2, u2, hs, hr, ss, sr,
):
    y, z, head = position()
    core = lax.rem(head, 2)
    seq = y * NZ + z
    barrier = pltpu.get_barrier_semaphore()

    def on(core_index, action):
        @pl.when(core == core_index)
        def _():
            action()

    def greet(to):
        pl.semaphore_signal(barrier, inc=1, device_id=to, device_id_type=MESH)

    def greet_axes(ring, direct, n):
        for step in (1, -1):
            greet(shifted(y, z, head, ring, step))
        for t in range(1, n):
            greet(shifted(y, z, head, direct, t))

    for t in range(1, NH):
        greet((seq, wrap(head + t, NH)))
    on(0, lambda: greet_axes(1, 0, NY))
    on(1, lambda: greet_axes(0, 1, NZ))
    parts = [
        pltpu.make_async_copy(first_ref, acc, a_sem.at[0]),
        pltpu.make_async_copy(second_ref, acc2, a_sem.at[1]),
    ]
    for x in parts:
        x.start()
    wcopy = pltpu.make_async_copy(w_ref, wbuf, w_sem)
    wcopy.start()
    picks = [(n, v) for n, (_, v) in enumerate(chosen(slot_ref, SYS_BLOCKS, (2, 3)))]

    def compute(pair, y_step, arrived):
        def coords(m):
            a = wrap(z + pair[m // 4], NZ)
            return (
                jnp.where(core == 0, m % 4, wrap(y + y_step, NY)),
                jnp.where(core == 0, a, m),
            )

        def load_q(m):
            return q_ref[coords(m)]

        def store(m, out, total):
            at = coords(m)
            acc[at] = (acc[at] + acc2[at]) + out
            sums[at] = l_ref[at] + jnp.concatenate([total, jnp.zeros((8, HEAD - ROWS), F32)], axis=1)

        system_round(load_q, store, pool, picks, qtmp, sbuf, otmp, lbuf, arrived)

    half = ROWS // 2

    def ring(axis1):
        axis2 = 1 - axis1
        n1, n2 = (NY, NZ) if axis1 == 0 else (NZ, NY)
        c1, c2 = (y, z) if axis1 == 0 else (z, y)
        h = n1 // 2
        rb, rl = (rb_y, rl_y) if axis1 == 0 else (rb_z, rl_z)
        order = [wrap(c2 + t, n2) for t in list(range(n2 // 2, n2)) + list(range(0, n2 // 2))]

        def own(i, j):
            return acc[i, j] if axis1 == 0 else acc[j, i]

        def own_l(i):
            return sums.at[i] if axis1 == 0 else sums.at[:, i]

        def copy(d, k, j):
            if k == 0:
                src = far.at[j, pl.ds(d * half, half)]
                dst = rb.at[d, 0, j, pl.ds(d * half, half)]
            else:
                src = rb.at[d, k - 1, j]
                dst = rb.at[d, k, j]
            return pltpu.make_async_remote_copy(
                src_ref=src, dst_ref=dst, send_sem=s1.at[d, k, j], recv_sem=r1.at[d, k, j],
                device_id=shifted(y, z, head, axis1, 1 - 2 * d), device_id_type=MESH,
            )

        def copy_l(d, k):
            s = 1 - 2 * d
            src = own_l(wrap(c1 + s * (h - k), n1)) if k == d else rl.at[d, k - 1]
            return pltpu.make_async_remote_copy(
                src_ref=src, dst_ref=rl.at[d, k], send_sem=t1.at[d, k], recv_sem=u1.at[d, k],
                device_id=shifted(y, z, head, axis1, s), device_id_type=MESH,
            )

        def begin():
            for j in order:
                far[j] = own(wrap(c1 + h, n1), j).astype(BF16)
                for d in (0, 1):
                    copy(d, 0, j).start()
            copy_l(0, 0).start()

        def step(d, k):
            to = wrap(c1 + (1 - 2 * d) * (h - k), n1)
            for j in order:
                copy(d, k - 1, j).wait_recv()
                here = own(to, j)
                if k == 1:
                    a = pl.ds(d * half, half)
                    b = pl.ds((1 - d) * half, half)
                    there = rb[d, 0, j, a].astype(F32)
                    rb[d, 0, j, a] = (there + here[d * half : (d + 1) * half]).astype(BF16)
                    rb[d, 0, j, b] = here[(1 - d) * half : (2 - d) * half].astype(BF16)
                else:
                    rb[d, k - 1, j] = (rb[d, k - 1, j].astype(F32) + here).astype(BF16)
                copy(d, k, j).start()
            if k > d:
                copy_l(d, k - 1).wait_recv()
                rl[d, k - 1] = rl[d, k - 1] + own_l(to)[...]
            copy_l(d, k).start()

        def direct(t):
            return pltpu.make_async_remote_copy(
                src_ref=part1.at[t], dst_ref=rb2.at[t], send_sem=s2.at[t], recv_sem=r2.at[t],
                device_id=shifted(y, z, head, axis2, t), device_id_type=MESH,
            )

        def direct_l(t):
            return pltpu.make_async_remote_copy(
                src_ref=lpart1.at[t], dst_ref=rl2.at[t], send_sem=t2.at[t], recv_sem=u2.at[t],
                device_id=shifted(y, z, head, axis2, t), device_id_type=MESH,
            )

        def final():
            turns = sorted(range(1, n2), key=lambda t: -min(t, n2 - t)) + [0]
            for n, t in enumerate(turns):
                j = wrap(c2 + t, n2)
                for d in (0, 1):
                    copy(d, h - 1, j).wait_recv()
                v = own(c1, j) + rb[0, h - 1, j].astype(F32) + rb[1, h - 1, j].astype(F32)
                if t == 0:
                    mine[...] = v
                else:
                    part1[t] = v.astype(BF16)
                    direct(t).start()
            for d in (0, 1):
                copy_l(d, h - 1).wait_recv()
            for t in turns:
                j = wrap(c2 + t, n2)
                at = (c1, j) if axis1 == 0 else (j, c1)
                v = sums[at] + rl[0, h - 1, j] + rl[1, h - 1, j]
                if t == 0:
                    small[...] = v
                else:
                    lpart1[t] = v
                    direct_l(t).start()
            v = mine[...]
            w = small[...]
            for t in turns[:-1]:
                direct(t).wait_recv()
                v = v + rb2[t].astype(F32)
            for t in turns[:-1]:
                direct_l(t).wait_recv()
                w = w + rl2[t]
            mine[...] = v
            small[...] = w
            for d in (0, 1):
                for k in range(h):
                    for j in order:
                        copy(d, k, j).wait_send()
                    if k >= d:
                        copy_l(d, k).wait_send()
            for t in turns[:-1]:
                direct(t).wait_send()
                direct_l(t).wait_send()

        return begin, step, final

    def steps(axis1, pairs):
        step = ring(axis1)[1]
        for d, k in pairs:
            step(d, k)

    def in_round(r, index, core_index, action):
        @pl.when((r == index) & (core == core_index))
        def _():
            action()

    def start(axis1, direct):
        pl.semaphore_wait(barrier, NH - 1 + 2 + direct - 1)
        ring(axis1)[0]()

    def arrived_in(r):
        @pl.when(r == 0)
        def _():
            for x in parts:
                x.wait()

    def one_round(r, _):
        y_step = jnp.where(r == 0, 2, jnp.where(r == 1, 1, jnp.where(r == 2, -1, 0)))
        compute((r - 4, 3 - r), y_step, lambda: arrived_in(r))
        in_round(r, 0, 0, lambda: start(1, NY))
        in_round(r, 0, 1, lambda: start(0, NZ))
        for k in range(1, 4):
            in_round(r, k, 0, lambda: steps(1, ((0, k), (1, k))))
        in_round(r, 1, 1, lambda: steps(0, ((0, 1),)))
        in_round(r, 2, 1, lambda: steps(0, ((1, 1),)))
        return 0

    lax.fori_loop(0, 4, one_round, 0)
    on(0, lambda: ring(1)[2]())
    on(1, lambda: ring(0)[2]())

    sums = jnp.transpose(jnp.concatenate([small[...], jnp.zeros((HEAD - 8, HEAD), F32)], axis=0))
    att = []
    for h in range(HEADS):
        den = sums[:ROWS, h : h + 1] + lloc[:, cols(h)]
        att.append(((mine[:, cols(h)] + oloc[:, cols(h)]) / den).astype(BF16))
    att = jnp.concatenate(att, axis=1)
    low = dot(att, down_ref[...])
    low_hi = low.astype(BF16)
    low_lo = (low - low_hi.astype(F32)).astype(BF16)
    low_lo2 = (low - low_hi.astype(F32) - low_lo.astype(F32)).astype(BF16)
    wcopy.wait()
    sends = {}
    for t in (4, 3, 5, 2, 6, 1, 7, 0):
        to = wrap(head + t, NH)
        odd = lax.rem(to, 2)
        at = pl.ds(pl.multiple_of(to * CHUNK - odd * (HEAD // 2), HEAD), PADDED)
        u = up_ref[:, at]
        v = dot(att, wbuf[:, at]) + (dot(low_hi, u) + dot(low_lo, u) + dot(low_lo2, u))
        v = jnp.where(odd == 1, v[:, HEAD // 2 :], v[:, :CHUNK])
        if t == 0:
            pmine[...] = v
            continue
        chunk[t - 1] = v.astype(BF16)
        x = pltpu.make_async_remote_copy(
            src_ref=chunk.at[t - 1], dst_ref=rchunk.at[t - 1], send_sem=hs.at[t - 1], recv_sem=hr.at[t - 1],
            device_id=(seq, to), device_id_type=MESH,
        )
        x.start()
        sends[t] = x
    p = pmine[...]
    for t in (1, 7, 2, 6, 3, 5, 4):
        sends[t].wait_recv()
        p = p + rchunk[t - 1].astype(F32)

    res = res_ref[...].astype(F32)
    gain = gain_ref[...]
    vhw = vhw_ref[...]
    pg = p * gain
    parts = [p * p, res * res, res * pg, pg * pg, res * vhw, pg * vhw]
    lane = lax.broadcasted_iota(jnp.int32, (ROWS, HEAD), 1)
    packed = jnp.zeros((ROWS, HEAD), F32)
    for i, v in enumerate(parts):
        packed = jnp.where(lane == i, jnp.sum(v, axis=1, keepdims=True), packed)
    packed = jnp.concatenate([packed, jnp.zeros((HEAD - ROWS, HEAD), F32)], axis=0)
    small[...] = jnp.transpose(packed)[:8]
    sends2 = []
    for t in range(1, NH):
        x = pltpu.make_async_remote_copy(
            src_ref=small, dst_ref=rsmall.at[t - 1], send_sem=ss.at[t - 1], recv_sem=sr.at[t - 1],
            device_id=(seq, wrap(head + t, NH)), device_id_type=MESH,
        )
        x.start()
        sends2.append(x)
    total = small[...]
    for t in range(1, NH):
        sends2[t - 1].wait_recv()
        total = total + rsmall[t - 1]
    sq, res2, rpg, pg2, rw, pgw = [total[i : i + 1] for i in range(6)]
    r = lax.rsqrt(sq / MODEL_WIDTH + EPS)
    power = res2 + 2.0 * r * rpg + r * r * pg2
    value = (rw + r * pgw) * lax.rsqrt(power / MODEL_WIDTH + EPS)
    for i in range(4):
        val_ref[i : i + 1, :] = value[:, i * 16 : (i + 1) * 16]
    rcol = jnp.transpose(jnp.broadcast_to(r, (HEAD, HEAD)))[:ROWS, :1]
    hid_ref[...] = (res + pg * rcol).astype(BF16)
    for x in list(sends.values()) + sends2:
        x.wait_send()


def local(
    queries, incoming_key_value, prefix_key_value_pool, response_key_value, residual, lengths,
    rollout_task_map, slot_block_table, output_projection_weight, adapter_down_weight,
    adapter_up_weight, post_norm_gain, value_head_weight,
):
    vmem = pl.BlockSpec(memory_space=pltpu.VMEM)
    smem = pl.BlockSpec(memory_space=pltpu.SMEM)
    hbm = pl.BlockSpec(memory_space=pltpu.HBM)
    dma = pltpu.SemaphoreType.DMA
    sds = jax.ShapeDtypeStruct
    devices = NY * NZ
    rows_all = devices * ROWS
    pool_buf = pltpu.VMEM((2, 8, 512, 256), BF16)
    round_bufs = [
        pltpu.VMEM((8 * ROWS, WIDTH), BF16),
        pltpu.VMEM((2, 512, 512), F32),
        pltpu.VMEM((8 * ROWS, WIDTH), F32),
        pltpu.VMEM((8 * ROWS, WIDTH), F32),
    ]

    qall, acc, sums, oloc, lloc, table = pl.pallas_call(
        gather_kernel,
        out_shape=(
            sds((NY, NZ, ROWS, WIDTH), BF16),
            sds((NY, NZ, ROWS, WIDTH), F32),
            sds((NY, NZ, 8, HEAD), F32),
            sds((ROWS, WIDTH), F32),
            sds((ROWS, WIDTH), F32),
            sds((16, HEAD), jnp.int32),
        ),
        in_specs=[smem, smem, vmem, vmem, vmem, hbm, hbm],
        out_specs=(vmem, hbm, vmem, vmem, vmem, vmem),
        scratch_shapes=[
            pltpu.VMEM((4, 2, 2048, 256), BF16),
            pool_buf,
            pltpu.VMEM((NY, NZ, ROWS, WIDTH), F32),
            *round_bufs,
            dma((4,)),
            dma(()),
            dma((NY, NZ)),
            dma((2, NZ // 2)),
            dma((2, NZ // 2)),
            dma((2, NZ, NZ // 2)),
            dma((2, NZ, NZ // 2)),
        ],
        compiler_params=pltpu.CompilerParams(
            collective_id=0, has_side_effects=True, vmem_limit_bytes=K1_MIB * MIB
        ),
        name="gather_queries",
    )(
        lengths, slot_block_table, queries.reshape(ROWS, WIDTH), incoming_key_value,
        rollout_task_map, response_key_value, prefix_key_value_pool,
    )

    rc = 1024
    acc2, sums2, chosen_blocks = pl.pallas_call(
        functools.partial(prefix_kernel, rc),
        out_shape=(
            sds((rows_all, WIDTH), F32),
            sds((devices, 8, HEAD), F32),
            sds((2, 2, 512, 256), BF16),
        ),
        in_specs=[smem, smem, vmem, hbm, vmem],
        out_specs=(hbm, vmem, vmem),
        scratch_shapes=[
            pool_buf,
            pltpu.VMEM((rows_all, WIDTH), F32),
            pltpu.VMEM((rows_all, WIDTH), F32),
            pltpu.VMEM((2, rc, 512), F32),
            pltpu.VMEM((2, GROUP * 16, WIDTH), BF16),
            pltpu.VMEM((GROUP * 16, WIDTH), F32),
            pltpu.VMEM((GROUP * 16, WIDTH), F32),
            pltpu.SMEM((16,), jnp.int32),
            pltpu.SMEM((24,), jnp.int32),
            pltpu.SMEM((24,), jnp.int32),
            pltpu.SMEM((24,), jnp.int32),
            dma(()),
            dma(()),
        ],
        compiler_params=pltpu.CompilerParams(vmem_limit_bytes=K2_MIB * MIB),
        name="prefix_attention",
    )(
        slot_block_table, table, qall.reshape(rows_all, WIDTH), prefix_key_value_pool,
        sums.reshape(devices, 8, HEAD),
    )

    hidden, values = pl.pallas_call(
        finish_kernel,
        out_shape=(sds((ROWS, CHUNK), BF16), sds((4, 16), F32)),
        in_specs=[smem] + [vmem] * 6 + [hbm] * 3 + [vmem] * 4,
        out_specs=(vmem, vmem),
        scratch_shapes=[
            pltpu.VMEM((WIDTH, MODEL_WIDTH), BF16),
            pltpu.VMEM((NY, NZ, ROWS, WIDTH), F32),
            pltpu.VMEM((NY, NZ, ROWS, WIDTH), F32),
            pltpu.VMEM((NY, NZ, 8, HEAD), F32),
            pltpu.VMEM((NZ, ROWS, WIDTH), BF16),
            *round_bufs,
            pltpu.VMEM((NZ, ROWS, WIDTH), BF16),
            pltpu.VMEM((NZ, 8, HEAD), F32),
            pltpu.VMEM((ROWS, WIDTH), F32),
            pltpu.VMEM((ROWS, CHUNK), F32),
            pltpu.VMEM((2, NY // 2, NZ, ROWS, WIDTH), BF16),
            pltpu.VMEM((2, NZ // 2, NY, ROWS, WIDTH), BF16),
            pltpu.VMEM((2, NY // 2, NZ, 8, HEAD), F32),
            pltpu.VMEM((2, NZ // 2, NY, 8, HEAD), F32),
            pltpu.VMEM((NZ, ROWS, WIDTH), BF16),
            pltpu.VMEM((NZ, 8, HEAD), F32),
            pltpu.VMEM((NH - 1, ROWS, CHUNK), BF16),
            pltpu.VMEM((NH - 1, ROWS, CHUNK), BF16),
            pltpu.VMEM((8, HEAD), F32),
            pltpu.VMEM((NH - 1, 8, HEAD), F32),
            dma(()),
            dma((2,)),
            dma((2, NZ // 2, NZ)),
            dma((2, NZ // 2, NZ)),
            dma((2, NZ // 2)),
            dma((2, NZ // 2)),
            dma((NZ,)),
            dma((NZ,)),
            dma((NZ,)),
            dma((NZ,)),
            dma((NH - 1,)),
            dma((NH - 1,)),
            dma((NH - 1,)),
            dma((NH - 1,)),
        ],
        compiler_params=pltpu.CompilerParams(
            collective_id=1, has_side_effects=True, vmem_limit_bytes=K3_MIB * MIB
        ),
        name="reduce_and_project",
    )(
        slot_block_table, sums2.reshape(NY, NZ, 8, HEAD), qall, oloc, lloc,
        residual.reshape(ROWS, CHUNK), chosen_blocks, acc, acc2.reshape(NY, NZ, ROWS, WIDTH),
        output_projection_weight,
        adapter_down_weight, adapter_up_weight, post_norm_gain.reshape(1, CHUNK),
        value_head_weight.reshape(1, CHUNK),
    )
    return hidden.reshape(residual.shape), values


def solution(mesh):
    placed = (
        P("seq", None, "head"),
        P(None, "seq", None, "head"),
        P(None, "seq", None, "head"),
        P(None, "seq", None, "head"),
        P("seq", None, "head"),
        P("seq"),
        P(),
        P("seq"),
        P("head", None),
        P("head", None),
        P(),
        P("head"),
        P("head"),
    )
    return jax.shard_map(
        local,
        mesh=mesh,
        in_specs=placed,
        out_specs=(P("seq", None, "head"), P("seq", None)),
        check_vma=False,
    )
```

```python
import functools

import jax
import jax.numpy as jnp
from jax import lax
from jax.experimental import pallas as pl
from jax.experimental.pallas import tpu as pltpu
from jax.sharding import PartitionSpec as P

MODEL_WIDTH = 4608
HEAD = 128
SYS_BLOCKS = 64
PROMPT_BLOCKS = 16
EPS = 1e-06
C1 = 144.0 ** (-0.5) / 50.0
C2 = 50.0 * 1.4426950408889634

NY, NZ, NH = 4, 8, 8
ROWS = 64
WIDTH = 512
HEADS = 4
CHUNK = 576
GROUP = 12
FAR_FIRST = (4, 3, 5, 2, 6, 1, 7, 0)
PADDED = 640
MIB = 1 << 20
K1_MIB, K2_MIB, K3_MIB = 58, 58, 58
MESH = pl.DeviceIdType.MESH
F32 = jnp.float32
BF16 = jnp.bfloat16


def weight_of(scores):
    return jnp.exp2(jnp.tanh(scores * C1) * C2)


def dot_t(a, b):
    return lax.dot_general(a, b, (((1,), (1,)), ((), ())), preferred_element_type=F32)


def dot(a, b):
    return jnp.dot(a, b, preferred_element_type=F32)


def lane_sum(p):
    total = p[:, :HEAD]
    for i in range(1, p.shape[1] // HEAD):
        total = total + p[:, i * HEAD : (i + 1) * HEAD]
    return total


def position():
    seq = lax.axis_index("seq")
    head = lax.axis_index("head")
    return lax.div(seq, NZ), lax.rem(seq, NZ), head


def wrap(v, n):
    return lax.rem(v + 2 * n, n)


def shifted(y, z, head, axis, step):
    if axis == 0:
        return (wrap(y + step, NY) * NZ + z, head)
    return (y * NZ + wrap(z + step, NZ), head)


def cols(h):
    return slice(h * HEAD, (h + 1) * HEAD)


def chosen(slot_ref, sys_blocks, ranks):
    found = [jnp.int32(0) for _ in ranks]
    seen = jnp.int32(0)
    for i in range(slot_ref.shape[0]):
        is_sys = (slot_ref[i] < sys_blocks).astype(jnp.int32)
        for n, rank in enumerate(ranks):
            found[n] = found[n] + i * is_sys * (seen == rank).astype(jnp.int32)
        seen = seen + is_sys
    return [(f, jnp.where(seen > rank, 1.0, 0.0)) for f, rank in zip(found, ranks)]


def head_picker():
    lane = lax.broadcasted_iota(jnp.int32, (8, WIDTH), 1)
    row = lax.broadcasted_iota(jnp.int32, (8, WIDTH), 0)
    return jnp.where(lax.div(lane, HEAD) == row, 1.0, 0.0).astype(BF16)


def head_sums(picker, lanes):
    hi = lanes.astype(BF16)
    lo = (lanes - hi.astype(F32)).astype(BF16)
    return dot_t(picker, hi) + dot_t(picker, lo)


def system_round(count, load_q, store, pool, picks, qtmp, sbuf, otmp, lbuf, arrived=None):
    n = count * ROWS
    for m in range(count):
        qtmp[m * ROWS : (m + 1) * ROWS, :] = load_q(m)
    (b0, v0), (b1, v1) = picks

    def score(h, b):
        return dot_t(qtmp[:n, cols(h)], pool[0, b, :, cols(h // 2)])

    sbuf[0, :n] = score(0, b0)
    for h in range(HEADS):
        g = h // 2
        sbuf[1, :n] = score(h, b1)
        p0 = weight_of(sbuf[0, :n])
        l0 = lane_sum(p0)
        o0 = dot(p0.astype(BF16), pool[1, b0, :, cols(g)])
        if h < HEADS - 1:
            sbuf[0, :n] = score(h + 1, b0)
        p1 = weight_of(sbuf[1, :n])
        l1 = lane_sum(p1)
        o1 = dot(p1.astype(BF16), pool[1, b1, :, cols(g)])
        otmp[:n, cols(h)] = o0 * v0 + o1 * v1
        lbuf[:n, cols(h)] = l0 * v0 + l1 * v1
    total = head_sums(head_picker(), lbuf[:n])
    if arrived is not None:
        arrived()
    for m in range(count):
        at = slice(m * ROWS, (m + 1) * ROWS)
        store(m, otmp[at, :], total[:, at])


def gather_kernel(
    len_ref, slot_ref, q_ref, inc_ref, map_ref, resp_ref, pool_ref,
    qall, acc_out, sums, oloc, lloc, table,
    cache, pool, acc, qtmp, sbuf, otmp, lbuf, load_sem, pool_sem, acc_sem, s1, r1, s2, r2,
):
    y, z, head = position()
    core = lax.rem(head, 2)

    barrier = pltpu.get_barrier_semaphore()

    def greet(axis, step):
        pl.semaphore_signal(
            barrier, inc=1, device_id=shifted(y, z, head, axis, step), device_id_type=MESH
        )

    for axis in (0, 1):
        for step in (1, -1):
            greet(axis, step)

    @pl.when(core == 1)
    def _():
        greet(1, 2)
        greet(1, -2)

    loads = []
    for i in range(4):
        c = pltpu.make_async_copy(resp_ref.at[:, i], cache.at[i], load_sem.at[i])
        c.start()
        loads.append(c)
    pool_load = pltpu.make_async_copy(pool_ref, pool, pool_sem)
    pool_load.start()
    qall[y, z] = q_ref[...]
    picks = chosen(slot_ref, SYS_BLOCKS, (0, 1))

    @pl.when(core == 0)
    def _():
        pl.semaphore_wait(barrier, 4)

    @pl.when(core == 1)
    def _():
        pl.semaphore_wait(barrier, 6)

    def list_members():
        across = jnp.broadcast_to(map_ref[...].astype(F32), (HEAD, HEAD))
        task = jnp.transpose(across)
        row = lax.broadcasted_iota(jnp.int32, (HEAD, HEAD), 0)
        lane = lax.broadcasted_iota(jnp.int32, (HEAD, HEAD), 1)
        earlier = jnp.where((task == across) & (lane < row), 1.0, 0.0)
        rank = jnp.sum(earlier, axis=1, keepdims=True)
        spot = jnp.where(rank == lane.astype(F32), 1.0, 0.0).astype(BF16)
        mine = across[:16] == row[:16].astype(F32)
        ids = jnp.where(mine, lane[:16].astype(F32), 0.0).astype(BF16)
        count = jnp.sum(jnp.where(mine, 1.0, 0.0), axis=1, keepdims=True)
        table[...] = jnp.where(lane[:16] == HEAD - 1, count, dot(ids, spot)).astype(jnp.int32)

    def attend(i):
        loads[i].wait()
        length = len_ref[i]
        rows = slice(i * 16, (i + 1) * 16)

        none = jnp.zeros((16, HEAD), BF16)
        lhs = jnp.concatenate(
            [
                jnp.concatenate(
                    [q_ref[rows, cols(h)], none] if h < 2 else [none, q_ref[rows, cols(h)]], axis=1
                )
                for h in range(HEADS)
            ],
            axis=0,
        )
        p = weight_of(dot_t(lhs, inc_ref[0, i]))
        n = lax.rem(lax.broadcasted_iota(jnp.int32, p.shape, 0), 16)
        m = lax.broadcasted_iota(jnp.int32, p.shape, 1)
        p = jnp.where(m <= n, p, 0.0)
        total = jnp.zeros((64, HEAD), F32)
        own = jnp.sum(p, axis=1, keepdims=True)
        out = dot(p.astype(BF16), inc_ref[1, i])
        for part in range(4):
            keys = slice(part * 512, (part + 1) * 512)
            p = weight_of(dot_t(lhs, cache[i, 0, keys, :]))
            where = lax.broadcasted_iota(jnp.int32, p.shape, 1) + part * 512
            p = jnp.where(where < length, p, 0.0)
            total = total + lane_sum(p)
            out = out + dot(p.astype(BF16), cache[i, 1, keys, :])
        wide = jnp.broadcast_to(jnp.sum(total, axis=1, keepdims=True) + own, (64, HEAD))
        for h in range(HEADS):
            at = slice(h * 16, (h + 1) * 16)
            oloc[rows, cols(h)] = out[at, cols(h // 2)]
            lloc[rows, cols(h)] = wide[at]

    def copies(axis1):
        axis2 = 1 - axis1
        n1, n2 = (NY, NZ) if axis1 == 0 else (NZ, NY)
        c1, c2 = (y, z) if axis1 == 0 else (z, y)
        h1, h2 = n1 // 2, n2 // 2
        offsets = [0]
        for k in range(1, h1):
            offsets += [-k, k]
        offsets.append(h1)

        def piece(i1, i2, part):
            a, b = (i1, i2) if axis1 == 0 else (i2, i1)
            view = qall.at[a, b]
            return view if part is None else view.at[pl.ds(part * (ROWS // 2), ROWS // 2)]

        def first(d, k):
            s = 1 - 2 * d
            if h1 == 2:
                origin, by = k, 1
            else:
                origin, by = 2 * (k // 2), 1 + k % 2
            view = piece(wrap(c1 - s * origin, n1), c2, d if k == h1 - 1 else None)
            return pltpu.make_async_remote_copy(
                src_ref=view, dst_ref=view, send_sem=s1.at[d, k], recv_sem=r1.at[d, k],
                device_id=shifted(y, z, head, axis1, s * by), device_id_type=MESH,
            )

        def second(j, d, k):
            s = 1 - 2 * d
            view = piece(wrap(c1 + offsets[j], n1), wrap(c2 - s * k, n2), d if k == h2 - 1 else None)
            return pltpu.make_async_remote_copy(
                src_ref=view, dst_ref=view, send_sem=s2.at[d, j, k], recv_sem=r2.at[d, j, k],
                device_id=shifted(y, z, head, axis2, s), device_id_type=MESH,
            )

        def spread(j):
            for e in (0, 1):
                second(j, e, 0).start()

        def phase1(work):
            both = (0, 1)
            if h1 == 2:
                for d in both:
                    first(d, 0).start()
                spread(0)
                attend(work[0])
                for d in both:
                    first(d, 0).wait_recv()
                    first(d, 1).start()
                for d in both:
                    spread(1 + d)
                attend(work[1])
                for d in both:
                    first(d, 1).wait_recv()
                spread(n1 - 1)
            else:
                for k in (1, 0):
                    for d in both:
                        first(d, k).start()
                spread(0)
                attend(work[0])
                attend(work[1])
                for d in both:
                    first(d, 1).wait_recv()
                    first(d, 3).start()
                    first(d, 2).start()
                for d in both:
                    first(d, 0).wait_recv()
                    spread(1 + d)
                for d in both:
                    spread(3 + d)
            attend(work[2])
            attend(work[3])
            if h1 != 2:
                for d in both:
                    first(d, 2).wait_recv()
                    spread(5 + d)
                for d in both:
                    first(d, 3).wait_recv()
                spread(n1 - 1)

        def forward(k):
            for j in range(n1):
                for d in (0, 1):
                    second(j, d, k).wait_recv()
                    if k < h2 - 1:
                        second(j, d, k + 1).start()

        def drain():
            for k in range(h1):
                for d in (0, 1):
                    first(d, k).wait_send()
            for k in range(h2):
                for j in range(n1):
                    for d in (0, 1):
                        second(j, d, k).wait_send()

        return phase1, forward, drain

    def on(core_index, action):
        @pl.when(core == core_index)
        def _():
            action()

    def start0():
        copies(0)[0]((0, 1, 2, 3))
        list_members()

    def start1():
        copies(1)[0]((0, 1, 2, 3))
        list_members()

    on(0, start0)
    on(1, start1)
    pool_load.wait()

    def keep(at):
        return pltpu.make_async_copy(acc.at[at], acc_out.at[at], acc_sem.at[at])

    def compute(count, unit):
        def coords(m):
            u = unit + m // 4
            k = lax.div(u, 2)
            odd = lax.rem(u, 2)
            column = jnp.where(odd == 1, -1 - k, k)
            row = jnp.where(k == 1, -1, jnp.where(k == 2, 1, jnp.where(k == 3, 2, 0)))
            return (
                jnp.where(core == 0, m % 4, wrap(y + row, NY)),
                jnp.where(core == 0, wrap(z + column, NZ), odd * 4 + m % 4),
            )

        def load_q(m):
            return qall[coords(m)]

        def store(m, out, total):
            at = coords(m)
            acc[at] = out
            keep(at).start()
            sums[at] = jnp.concatenate([total, jnp.zeros((8, HEAD - ROWS), F32)], axis=1)

        system_round(count, load_q, store, pool, picks, qtmp, sbuf, otmp, lbuf)

    def in_round(r, index, core_index, action):
        @pl.when((r == index) & (core == core_index))
        def _():
            action()

    def one_round(r, _):
        @pl.when((r == 0) | (r == 4))
        def _():
            compute(4, jnp.where(r == 0, 0, 7))

        @pl.when((r > 0) & (r < 4))
        def _():
            compute(8, 2 * r - 1)

        for k in range(4):
            in_round(r, k, 0, lambda: copies(0)[1](k))
        in_round(r, 0, 1, lambda: copies(1)[1](0))
        in_round(r, 2, 1, lambda: copies(1)[1](1))
        return 0

    lax.fori_loop(0, 5, one_round, 0)
    on(0, lambda: copies(0)[2]())
    on(1, lambda: copies(1)[2]())
    for a in range(NY):
        for b in range(NZ):
            keep((a, b)).wait()


def prefix_kernel(
    rc, slot_ref, table_ref, q_ref, pool_hbm, lin_ref, acc_out, l_ref, sel,
    pool_ref, acc, lanes, sbuf, qbuf, obuf, lbuf, system, item_slot, item_prompt, item_part, pool_sem, acc_sem,
):
    pool_load = pltpu.make_async_copy(pool_hbm, pool_ref, pool_sem)
    pool_load.start()
    slots = slot_ref.shape[0]
    total_rows = q_ref.shape[0]
    chunks = total_rows // rc

    for i in range(8):
        system[i] = 0
    count = jnp.int32(0)
    items_p = jnp.int32(0)
    for i in range(slots):
        logical = slot_ref[i]
        system[count] = i
        count = count + (logical < SYS_BLOCKS).astype(jnp.int32)
        p = lax.div(jnp.maximum(logical - SYS_BLOCKS, 0), PROMPT_BLOCKS)
        n = jnp.where(logical < SYS_BLOCKS, 0, table_ref[p, HEAD - 1])
        for c in range(2):
            item_slot[items_p] = i
            item_prompt[items_p] = p
            item_part[items_p] = c
            items_p = items_p + (n > c * GROUP).astype(jnp.int32)
    count = jnp.maximum(count - 4, 0)

    def rows_of(c):
        return pl.ds(pl.multiple_of(c * rc, rc), rc)

    def score(item, h):
        c = lax.div(item, count)
        b = system[4 + lax.rem(item, count)]
        return dot_t(q_ref[rows_of(c), cols(h)], pool_ref[0, b, :, cols(h // 2)])

    acc[...] = jnp.zeros_like(acc)
    lanes[...] = jnp.zeros_like(lanes)
    pool_load.wait()
    for n in range(2):
        for kv in range(2):
            sel[kv, n] = pool_ref[kv, system[2 + n]]

    @pl.when(count > 0)
    def _():
        items = count * chunks
        sbuf[0] = score(0, 0)

        def step(item, _):
            rows = rows_of(lax.div(item, count))
            turn = lax.rem(item, count)
            b = system[4 + turn]
            following = jnp.minimum(item + 1, items - 1)
            for h in range(HEADS):
                if h < HEADS - 1:
                    sbuf[(h + 1) % 2] = score(item, h + 1)
                else:
                    sbuf[0] = score(following, 0)
                p = weight_of(sbuf[h % 2])
                part = lane_sum(p)
                out = dot(p.astype(BF16), pool_ref[1, b, :, cols(h // 2)])
                lanes[rows, cols(h)] += part
                acc[rows, cols(h)] += out
            return 0

        lax.fori_loop(0, items, step, 0)

    rows_g = GROUP * 16

    def pick(k, turn):
        p = item_prompt[k]
        c = item_part[k]
        for m in range(GROUP):
            r = table_ref[p, c * GROUP + m]
            qbuf[turn, m * 16 : (m + 1) * 16, :] = q_ref[pl.ds(pl.multiple_of(r * 16, 16), 16), :]

    def member_score(k, turn, g):
        lhs = jnp.concatenate([qbuf[turn, :, cols(2 * g)], qbuf[turn, :, cols(2 * g + 1)]], axis=0)
        return dot_t(lhs, pool_ref[0, item_slot[k], :, cols(g)])

    def member_weights(k, g):
        w = weight_of(sbuf[g, : 2 * rows_g])
        part = lane_sum(w)
        out = dot(w.astype(BF16), pool_ref[1, item_slot[k], :, cols(g)])
        for j in range(2):
            at = slice(j * rows_g, (j + 1) * rows_g)
            obuf[:, cols(2 * g + j)] = out[at]
            lbuf[:, cols(2 * g + j)] = part[at]

    @pl.when(items_p > 0)
    def _():
        pick(0, 0)
        sbuf[0, : 2 * rows_g] = member_score(0, 0, 0)

        def one(k, _):
            turn = lax.rem(k, 2)
            following = jnp.minimum(k + 1, items_p - 1)
            sbuf[1, : 2 * rows_g] = member_score(k, turn, 1)
            pick(following, 1 - turn)
            member_weights(k, 0)
            sbuf[0, : 2 * rows_g] = member_score(following, 1 - turn, 0)
            member_weights(k, 1)
            p = item_prompt[k]
            c = item_part[k]
            n = table_ref[p, HEAD - 1]
            for m in range(GROUP):
                r = table_ref[p, c * GROUP + m]
                at = pl.ds(pl.multiple_of(r * 16, 16), 16)
                src = slice(m * 16, (m + 1) * 16)
                there = jnp.where(c * GROUP + m < n, 1.0, 0.0)
                acc[at, :] += obuf[src, :] * there
                lanes[at, :] += lbuf[src, :] * there
            return 0

        lax.fori_loop(0, items_p, one, 0)

    acc_store = pltpu.make_async_copy(acc, acc_out, acc_sem)
    acc_store.start()
    picker = head_picker()

    def finish(c, _):
        total = head_sums(picker, lanes[pl.ds(pl.multiple_of(c * 512, 512), 512), :])
        for m in range(8):
            l_ref[c * 8 + m] = lin_ref[c * 8 + m]
            l_ref[c * 8 + m, :, :ROWS] += total[:, m * ROWS : (m + 1) * ROWS]
        return 0

    lax.fori_loop(0, total_rows // 512, finish, 0)
    acc_store.wait()


def finish_kernel(
    slot_ref, l_ref, q_ref, oloc, lloc, res_ref, pool, first_ref, second_ref, w_ref, down_ref, up_ref, gain_ref, vhw_ref,
    hid_ref, val_ref,
    wbuf, acc, acc2, sums, far, qtmp, sbuf, otmp, lbuf, part1, lpart1, mine, pmine,
    rb_y, rb_z, rl_y, rl_z, rb2, rl2, chunk, rchunk, small, rsmall,
    w_sem, a_sem, s1, r1, t1, u1, s2, r2, t2, u2, hs, hr, ss, sr,
):
    y, z, head = position()
    core = lax.rem(head, 2)
    seq = y * NZ + z
    barrier = pltpu.get_barrier_semaphore()

    def on(core_index, action):
        @pl.when(core == core_index)
        def _():
            action()

    def greet(to):
        pl.semaphore_signal(barrier, inc=1, device_id=to, device_id_type=MESH)

    def greet_axes(ring, direct, n):
        for step in (1, -1):
            greet(shifted(y, z, head, ring, step))
        for t in range(1, n):
            greet(shifted(y, z, head, direct, t))

    for t in range(1, NH):
        greet((seq, wrap(head + t, NH)))
    on(0, lambda: greet_axes(1, 0, NY))
    on(1, lambda: greet_axes(0, 1, NZ))
    parts = [
        pltpu.make_async_copy(first_ref, acc, a_sem.at[0]),
        pltpu.make_async_copy(second_ref, acc2, a_sem.at[1]),
    ]
    for x in parts:
        x.start()
    wcopy = pltpu.make_async_copy(w_ref, wbuf, w_sem)
    wcopy.start()
    picks = [(n, v) for n, (_, v) in enumerate(chosen(slot_ref, SYS_BLOCKS, (2, 3)))]

    def compute(count, unit, arrived):
        def coords(m):
            u = unit + m // 4
            k = lax.div(u, 2)
            odd = lax.rem(u, 2)
            column = jnp.where(odd == 1, 3 - k, k - 4)
            row = jnp.where(k == 0, 2, jnp.where(k == 1, 1, jnp.where(k == 2, -1, 0)))
            place = jnp.where(odd == 0, FAR_FIRST[m % 4], FAR_FIRST[4 + m % 4])
            return (
                jnp.where(core == 0, m % 4, wrap(y + row, NY)),
                jnp.where(core == 0, wrap(z + column, NZ), wrap(z + place, NZ)),
            )

        def load_q(m):
            return q_ref[coords(m)]

        def store(m, out, total):
            at = coords(m)
            acc[at] = (acc[at] + acc2[at]) + out
            sums[at] = l_ref[at] + jnp.concatenate([total, jnp.zeros((8, HEAD - ROWS), F32)], axis=1)

        system_round(count, load_q, store, pool, picks, qtmp, sbuf, otmp, lbuf, arrived)

    half = ROWS // 2

    def ring(axis1):
        axis2 = 1 - axis1
        n1, n2 = (NY, NZ) if axis1 == 0 else (NZ, NY)
        c1, c2 = (y, z) if axis1 == 0 else (z, y)
        h = n1 // 2
        rb, rl = (rb_y, rl_y) if axis1 == 0 else (rb_z, rl_z)
        turns = sorted(range(1, n2), key=lambda t: -min(t, n2 - t)) + [0]
        order = [wrap(c2 + t, n2) for t in turns]

        def own(i, j):
            return acc[i, j] if axis1 == 0 else acc[j, i]

        def own_l(i):
            return sums.at[i] if axis1 == 0 else sums.at[:, i]

        def copy(d, k, j):
            if k == 0:
                src = far.at[j, pl.ds(d * half, half)]
                dst = rb.at[d, 0, j, pl.ds(d * half, half)]
            else:
                src = rb.at[d, k - 1, j]
                dst = rb.at[d, k, j]
            return pltpu.make_async_remote_copy(
                src_ref=src, dst_ref=dst, send_sem=s1.at[d, k, j], recv_sem=r1.at[d, k, j],
                device_id=shifted(y, z, head, axis1, 1 - 2 * d), device_id_type=MESH,
            )

        def copy_l(d, k):
            s = 1 - 2 * d
            src = own_l(wrap(c1 + s * (h - k), n1)) if k == d else rl.at[d, k - 1]
            return pltpu.make_async_remote_copy(
                src_ref=src, dst_ref=rl.at[d, k], send_sem=t1.at[d, k], recv_sem=u1.at[d, k],
                device_id=shifted(y, z, head, axis1, s), device_id_type=MESH,
            )

        def begin(js):
            for j in js:
                far[j] = own(wrap(c1 + h, n1), j).astype(BF16)
                for d in (0, 1):
                    copy(d, 0, j).start()

        def step_l(pairs):
            for d, k in pairs:
                if k > d:
                    copy_l(d, k - 1).wait_recv()
                    rl[d, k - 1] = rl[d, k - 1] + own_l(wrap(c1 + (1 - 2 * d) * (h - k), n1))[...]
                copy_l(d, k).start()

        def step(pairs, js):
            for j in js:
                for d, k in pairs:
                    copy(d, k - 1, j).wait_recv()
                    here = own(wrap(c1 + (1 - 2 * d) * (h - k), n1), j)
                    if k == 1:
                        a = pl.ds(d * half, half)
                        b = pl.ds((1 - d) * half, half)
                        there = rb[d, 0, j, a].astype(F32)
                        rb[d, 0, j, a] = (there + here[d * half : (d + 1) * half]).astype(BF16)
                        rb[d, 0, j, b] = here[(1 - d) * half : (2 - d) * half].astype(BF16)
                    else:
                        rb[d, k - 1, j] = (rb[d, k - 1, j].astype(F32) + here).astype(BF16)
                    copy(d, k, j).start()

        def direct(t):
            return pltpu.make_async_remote_copy(
                src_ref=part1.at[t], dst_ref=rb2.at[t], send_sem=s2.at[t], recv_sem=r2.at[t],
                device_id=shifted(y, z, head, axis2, t), device_id_type=MESH,
            )

        def direct_l(t):
            return pltpu.make_async_remote_copy(
                src_ref=lpart1.at[t], dst_ref=rl2.at[t], send_sem=t2.at[t], recv_sem=u2.at[t],
                device_id=shifted(y, z, head, axis2, t), device_id_type=MESH,
            )

        def final():
            for d in (0, 1):
                copy_l(d, h - 1).wait_recv()
            for t in turns:
                j = wrap(c2 + t, n2)
                at = (c1, j) if axis1 == 0 else (j, c1)
                v = sums[at] + rl[0, h - 1, j] + rl[1, h - 1, j]
                if t == 0:
                    small[...] = v
                else:
                    lpart1[t] = v
                    direct_l(t).start()
            for t in turns:
                j = wrap(c2 + t, n2)
                for d in (0, 1):
                    copy(d, h - 1, j).wait_recv()
                v = own(c1, j) + rb[0, h - 1, j].astype(F32) + rb[1, h - 1, j].astype(F32)
                if t == 0:
                    mine[...] = v
                else:
                    part1[t] = v.astype(BF16)
                    direct(t).start()
            w = small[...]
            for t in turns[:-1]:
                direct_l(t).wait_recv()
                w = w + rl2[t]
            small[...] = w
            v = mine[...]
            for t in turns[:-1]:
                direct(t).wait_recv()
                v = v + rb2[t].astype(F32)
            mine[...] = v

        def drain():
            for d in (0, 1):
                for k in range(h):
                    for j in order:
                        copy(d, k, j).wait_send()
                    if k >= d:
                        copy_l(d, k).wait_send()
            for t in turns[:-1]:
                direct(t).wait_send()
                direct_l(t).wait_send()

        return begin, step, step_l, final, drain, order

    def after0(r):
        begin, step, step_l, _, _, order = ring(1)
        if r == 0:
            pl.semaphore_wait(barrier, NH - 1 + 2 + NY - 1)
            step_l(((0, 0),))
            begin(order)
        else:
            step_l(((0, r), (1, r)))
            step(((0, r), (1, r)), order)

    def after1(r):
        begin, step, step_l, _, _, order = ring(0)
        a, b = order[:4], order[4:]
        if r == 0:
            pl.semaphore_wait(barrier, NH - 1 + 2 + NZ - 1)
            begin(a)
        elif r == 1:
            step_l(((0, 0),))
            begin(b)
            step(((0, 1),), a)
        elif r == 2:
            step_l(((0, 1),))
            step(((0, 1),), b)
            step(((1, 1),), a)
        else:
            step_l(((1, 1),))
            step(((1, 1),), b)

    def in_round(r, index, core_index, action):
        @pl.when((r == index) & (core == core_index))
        def _():
            action()

    def arrived_in(r):
        @pl.when(r == 0)
        def _():
            for x in parts:
                x.wait()

    def one_round(r, _):
        @pl.when((r == 0) | (r == 4))
        def _():
            compute(4, jnp.where(r == 0, 0, 7), lambda: arrived_in(r))

        @pl.when((r > 0) & (r < 4))
        def _():
            compute(8, 2 * r - 1, None)

        for k in range(4):
            in_round(r, k, 0, lambda: after0(k))
            in_round(r, k, 1, lambda: after1(k))
        return 0

    lax.fori_loop(0, 5, one_round, 0)
    on(0, lambda: ring(1)[3]())
    on(1, lambda: ring(0)[3]())

    rows_sum = jnp.transpose(jnp.concatenate([small[...], jnp.zeros((HEAD - 8, HEAD), F32)], axis=0))
    att = []
    for h in range(HEADS):
        den = rows_sum[:ROWS, h : h + 1] + lloc[:, cols(h)]
        att.append(((mine[:, cols(h)] + oloc[:, cols(h)]) / den).astype(BF16))
    att = jnp.concatenate(att, axis=1)
    low = dot_t(att, down_ref[...])
    low_hi = low.astype(BF16)
    low_lo = (low - low_hi.astype(F32)).astype(BF16)
    low_lo2 = (low - low_hi.astype(F32) - low_lo.astype(F32)).astype(BF16)
    low3 = jnp.concatenate([low_hi, low_lo, low_lo2], axis=1)
    wcopy.wait()
    def project(to):
        odd = lax.rem(to, 2)
        at = pl.ds(pl.multiple_of(to * CHUNK - odd * (HEAD // 2), HEAD), PADDED)
        u = up_ref[:, at]
        v = dot(att, wbuf[:, at]) + dot(low3, jnp.concatenate([u, u, u], axis=0))
        return jnp.where(odd == 1, v[:, HEAD // 2 :], v[:, :CHUNK])

    x_here = lax.div(head, 2)
    sends = []
    for t in (2, 1, 3, 0):
        chunk[t] = project(2 * wrap(x_here + t, NH // 2) + 1 - core).astype(BF16)
        x = pltpu.make_async_remote_copy(
            src_ref=chunk.at[t], dst_ref=rchunk.at[t], send_sem=hs.at[t], recv_sem=hr.at[t],
            device_id=(seq, 2 * x_here + 1 - core), device_id_type=MESH,
        )
        x.start()
        sends.append(x)
    across = {}
    for n, t in enumerate((2, 1, 3, 0)):
        v = project(2 * wrap(x_here + t, NH // 2) + core)
        sends[n].wait_recv()
        v = v + rchunk[t].astype(F32)
        if t == 0:
            pmine[...] = v
            continue
        chunk[3 + t] = v.astype(BF16)
        x = pltpu.make_async_remote_copy(
            src_ref=chunk.at[3 + t], dst_ref=rchunk.at[3 + t], send_sem=hs.at[3 + t], recv_sem=hr.at[3 + t],
            device_id=(seq, 2 * wrap(x_here + t, NH // 2) + core), device_id_type=MESH,
        )
        x.start()
        across[t] = x
        sends.append(x)
    p = pmine[...]
    for t in (1, 3, 2):
        across[t].wait_recv()
        p = p + rchunk[3 + t].astype(F32)

    res = res_ref[...].astype(F32)
    gain = gain_ref[...].reshape(1, CHUNK)
    vhw = vhw_ref[...].reshape(1, CHUNK)
    pg = p * gain
    terms = [p * p, res * res, res * pg, pg * pg, res * vhw, pg * vhw]
    lane = lax.broadcasted_iota(jnp.int32, (ROWS, HEAD), 1)
    packed = jnp.zeros((ROWS, HEAD), F32)
    for i, v in enumerate(terms):
        packed = jnp.where(lane == i, jnp.sum(v, axis=1, keepdims=True), packed)
    packed = jnp.concatenate([packed, jnp.zeros((HEAD - ROWS, HEAD), F32)], axis=0)
    small[...] = jnp.transpose(packed)[:8]
    sends2 = []
    for t in range(1, NH):
        x = pltpu.make_async_remote_copy(
            src_ref=small, dst_ref=rsmall.at[t - 1], send_sem=ss.at[t - 1], recv_sem=sr.at[t - 1],
            device_id=(seq, wrap(head + t, NH)), device_id_type=MESH,
        )
        x.start()
        sends2.append(x)
    total = small[...]
    for t in range(1, NH):
        sends2[t - 1].wait_recv()
        total = total + rsmall[t - 1]
    sq, res2, rpg, pg2, rw, pgw = [total[i : i + 1] for i in range(6)]
    r = lax.rsqrt(sq / MODEL_WIDTH + EPS)
    power = res2 + 2.0 * r * rpg + r * r * pg2
    value = (rw + r * pgw) * lax.rsqrt(power / MODEL_WIDTH + EPS)
    for i in range(4):
        val_ref[i : i + 1, :] = value[:, i * 16 : (i + 1) * 16]
    rcol = jnp.transpose(jnp.broadcast_to(r, (HEAD, HEAD)))[:ROWS, :1]
    hid_ref[...] = (res + pg * rcol).astype(BF16)
    for x in sends + sends2:
        x.wait_send()
    on(0, lambda: ring(1)[4]())
    on(1, lambda: ring(0)[4]())


def local(
    queries, incoming_key_value, prefix_key_value_pool, response_key_value, residual, lengths,
    rollout_task_map, slot_block_table, output_projection_weight, adapter_down_weight,
    adapter_up_weight, post_norm_gain, value_head_weight,
):
    vmem = pl.BlockSpec(memory_space=pltpu.VMEM)
    smem = pl.BlockSpec(memory_space=pltpu.SMEM)
    hbm = pl.BlockSpec(memory_space=pltpu.HBM)
    dma = pltpu.SemaphoreType.DMA
    sds = jax.ShapeDtypeStruct
    devices = NY * NZ
    rows_all = devices * ROWS
    pool_buf = pltpu.VMEM((2, 8, 512, 256), BF16)
    round_bufs = [
        pltpu.VMEM((8 * ROWS, WIDTH), BF16),
        pltpu.VMEM((2, 512, 512), F32),
        pltpu.VMEM((8 * ROWS, WIDTH), F32),
        pltpu.VMEM((8 * ROWS, WIDTH), F32),
    ]

    qall, acc, sums, oloc, lloc, table = pl.pallas_call(
        gather_kernel,
        out_shape=(
            sds((NY, NZ, ROWS, WIDTH), BF16),
            sds((NY, NZ, ROWS, WIDTH), F32),
            sds((NY, NZ, 8, HEAD), F32),
            sds((ROWS, WIDTH), F32),
            sds((ROWS, WIDTH), F32),
            sds((16, HEAD), jnp.int32),
        ),
        in_specs=[smem, smem, vmem, vmem, vmem, hbm, hbm],
        out_specs=(vmem, hbm, vmem, vmem, vmem, vmem),
        scratch_shapes=[
            pltpu.VMEM((4, 2, 2048, 256), BF16),
            pool_buf,
            pltpu.VMEM((NY, NZ, ROWS, WIDTH), F32),
            *round_bufs,
            dma((4,)),
            dma(()),
            dma((NY, NZ)),
            dma((2, NZ // 2)),
            dma((2, NZ // 2)),
            dma((2, NZ, NZ // 2)),
            dma((2, NZ, NZ // 2)),
        ],
        compiler_params=pltpu.CompilerParams(
            collective_id=0, has_side_effects=True, vmem_limit_bytes=K1_MIB * MIB
        ),
        name="gather_queries",
    )(
        lengths, slot_block_table, queries.reshape(ROWS, WIDTH), incoming_key_value,
        rollout_task_map.reshape(1, -1), response_key_value, prefix_key_value_pool,
    )

    rc = 1024
    acc2, sums2, chosen_blocks = pl.pallas_call(
        functools.partial(prefix_kernel, rc),
        out_shape=(
            sds((rows_all, WIDTH), F32),
            sds((devices, 8, HEAD), F32),
            sds((2, 2, 512, 256), BF16),
        ),
        in_specs=[smem, smem, vmem, hbm, vmem],
        out_specs=(hbm, vmem, vmem),
        scratch_shapes=[
            pool_buf,
            pltpu.VMEM((rows_all, WIDTH), F32),
            pltpu.VMEM((rows_all, WIDTH), F32),
            pltpu.VMEM((2, rc, 512), F32),
            pltpu.VMEM((2, GROUP * 16, WIDTH), BF16),
            pltpu.VMEM((GROUP * 16, WIDTH), F32),
            pltpu.VMEM((GROUP * 16, WIDTH), F32),
            pltpu.SMEM((16,), jnp.int32),
            pltpu.SMEM((24,), jnp.int32),
            pltpu.SMEM((24,), jnp.int32),
            pltpu.SMEM((24,), jnp.int32),
            dma(()),
            dma(()),
        ],
        compiler_params=pltpu.CompilerParams(vmem_limit_bytes=K2_MIB * MIB),
        name="prefix_attention",
    )(
        slot_block_table, table, qall.reshape(rows_all, WIDTH), prefix_key_value_pool,
        sums.reshape(devices, 8, HEAD),
    )

    hidden, values = pl.pallas_call(
        finish_kernel,
        out_shape=(sds((ROWS, CHUNK), BF16), sds((4, 16), F32)),
        in_specs=[smem] + [vmem] * 6 + [hbm] * 3 + [vmem] * 4,
        out_specs=(vmem, vmem),
        scratch_shapes=[
            pltpu.VMEM((WIDTH, MODEL_WIDTH), BF16),
            pltpu.VMEM((NY, NZ, ROWS, WIDTH), F32),
            pltpu.VMEM((NY, NZ, ROWS, WIDTH), F32),
            pltpu.VMEM((NY, NZ, 8, HEAD), F32),
            pltpu.VMEM((NZ, ROWS, WIDTH), BF16),
            *round_bufs,
            pltpu.VMEM((NZ, ROWS, WIDTH), BF16),
            pltpu.VMEM((NZ, 8, HEAD), F32),
            pltpu.VMEM((ROWS, WIDTH), F32),
            pltpu.VMEM((ROWS, CHUNK), F32),
            pltpu.VMEM((2, NY // 2, NZ, ROWS, WIDTH), BF16),
            pltpu.VMEM((2, NZ // 2, NY, ROWS, WIDTH), BF16),
            pltpu.VMEM((2, NY // 2, NZ, 8, HEAD), F32),
            pltpu.VMEM((2, NZ // 2, NY, 8, HEAD), F32),
            pltpu.VMEM((NZ, ROWS, WIDTH), BF16),
            pltpu.VMEM((NZ, 8, HEAD), F32),
            pltpu.VMEM((NH - 1, ROWS, CHUNK), BF16),
            pltpu.VMEM((NH - 1, ROWS, CHUNK), BF16),
            pltpu.VMEM((8, HEAD), F32),
            pltpu.VMEM((NH - 1, 8, HEAD), F32),
            dma(()),
            dma((2,)),
            dma((2, NZ // 2, NZ)),
            dma((2, NZ // 2, NZ)),
            dma((2, NZ // 2)),
            dma((2, NZ // 2)),
            dma((NZ,)),
            dma((NZ,)),
            dma((NZ,)),
            dma((NZ,)),
            dma((NH - 1,)),
            dma((NH - 1,)),
            dma((NH - 1,)),
            dma((NH - 1,)),
        ],
        compiler_params=pltpu.CompilerParams(
            collective_id=1, has_side_effects=True, vmem_limit_bytes=K3_MIB * MIB
        ),
        name="reduce_and_project",
    )(
        slot_block_table, sums2.reshape(NY, NZ, 8, HEAD), qall, oloc, lloc,
        residual.reshape(ROWS, CHUNK), chosen_blocks, acc, acc2.reshape(NY, NZ, ROWS, WIDTH),
        output_projection_weight,
        adapter_down_weight.T, adapter_up_weight, post_norm_gain, value_head_weight,
    )
    return hidden.reshape(residual.shape), values


def solution(mesh):
    placed = (
        P("seq", None, "head"),
        P(None, "seq", None, "head"),
        P(None, "seq", None, "head"),
        P(None, "seq", None, "head"),
        P("seq", None, "head"),
        P("seq"),
        P(),
        P("seq"),
        P("head", None),
        P("head", None),
        P(),
        P("head"),
        P("head"),
    )
    return jax.shard_map(
        local,
        mesh=mesh,
        in_specs=placed,
        out_specs=(P("seq", None, "head"), P("seq", None)),
        check_vma=False,
    )
```

```python
import functools

import jax
import jax.numpy as jnp
from jax import lax
from jax.experimental import pallas as pl
from jax.experimental.pallas import tpu as pltpu
from jax.sharding import PartitionSpec as P

MODEL_WIDTH = 4608
HEAD = 128
SYS_BLOCKS = 64
PROMPT_BLOCKS = 16
EPS = 1e-06
C1 = 144.0 ** (-0.5) / 50.0
C2 = 50.0 * 1.4426950408889634

NY, NZ, NH = 4, 8, 8
ROWS = 64
WIDTH = 512
HEADS = 4
CHUNK = 576
GROUP = 12
FAR_FIRST = (4, 3, 5, 2, 6, 1, 7, 0)
PADDED = 640
MIB = 1 << 20
K1_MIB, K2_MIB, K3_MIB = 58, 58, 58
MESH = pl.DeviceIdType.MESH
F32 = jnp.float32
BF16 = jnp.bfloat16


def weight_of(scores):
    return jnp.exp2(jnp.tanh(scores * C1) * C2)


def dot_t(a, b):
    return lax.dot_general(a, b, (((1,), (1,)), ((), ())), preferred_element_type=F32)


def dot(a, b):
    return jnp.dot(a, b, preferred_element_type=F32)


def lane_sum(p):
    total = p[:, :HEAD]
    for i in range(1, p.shape[1] // HEAD):
        total = total + p[:, i * HEAD : (i + 1) * HEAD]
    return total


def position():
    seq = lax.axis_index("seq")
    head = lax.axis_index("head")
    return lax.div(seq, NZ), lax.rem(seq, NZ), head


def wrap(v, n):
    return lax.rem(v + 2 * n, n)


def shifted(y, z, head, axis, step):
    if axis == 0:
        return (wrap(y + step, NY) * NZ + z, head)
    return (y * NZ + wrap(z + step, NZ), head)


def cols(h):
    return slice(h * HEAD, (h + 1) * HEAD)


def chosen(slot_ref, sys_blocks, ranks):
    found = [jnp.int32(0) for _ in ranks]
    seen = jnp.int32(0)
    for i in range(slot_ref.shape[0]):
        is_sys = (slot_ref[i] < sys_blocks).astype(jnp.int32)
        for n, rank in enumerate(ranks):
            found[n] = found[n] + i * is_sys * (seen == rank).astype(jnp.int32)
        seen = seen + is_sys
    return [(f, jnp.where(seen > rank, 1.0, 0.0)) for f, rank in zip(found, ranks)]


def head_picker():
    lane = lax.broadcasted_iota(jnp.int32, (8, WIDTH), 1)
    row = lax.broadcasted_iota(jnp.int32, (8, WIDTH), 0)
    return jnp.where(lax.div(lane, HEAD) == row, 1.0, 0.0).astype(BF16)


def head_sums(picker, lanes):
    hi = lanes.astype(BF16)
    lo = (lanes - hi.astype(F32)).astype(BF16)
    return dot_t(picker, hi) + dot_t(picker, lo)


def system_round(count, load_q, store, pool, picks, qtmp, sbuf, otmp, lbuf, arrived=None):
    n = count * ROWS
    for m in range(count):
        qtmp[m * ROWS : (m + 1) * ROWS, :] = load_q(m)
    (b0, v0), (b1, v1) = picks

    def score(h, b):
        return dot_t(qtmp[:n, cols(h)], pool[0, b, :, cols(h // 2)])

    sbuf[0, :n] = score(0, b0)
    for h in range(HEADS):
        g = h // 2
        sbuf[1, :n] = score(h, b1)
        p0 = weight_of(sbuf[0, :n])
        l0 = lane_sum(p0)
        o0 = dot(p0.astype(BF16), pool[1, b0, :, cols(g)])
        if h < HEADS - 1:
            sbuf[0, :n] = score(h + 1, b0)
        p1 = weight_of(sbuf[1, :n])
        l1 = lane_sum(p1)
        o1 = dot(p1.astype(BF16), pool[1, b1, :, cols(g)])
        otmp[:n, cols(h)] = o0 * v0 + o1 * v1
        lbuf[:n, cols(h)] = l0 * v0 + l1 * v1
    total = head_sums(head_picker(), lbuf[:n])
    if arrived is not None:
        arrived()
    for m in range(count):
        at = slice(m * ROWS, (m + 1) * ROWS)
        store(m, otmp[at, :], total[:, at])


def gather_kernel(
    len_ref, slot_ref, q_ref, inc_ref, map_ref, resp_ref, pool_ref,
    q_out, acc_out, sums, oloc, lloc, table,
    qall, cache, pool, acc, qtmp, sbuf, otmp, lbuf, load_sem, pool_sem, q_sem, acc_sem, s1, r1, s2, r2,
):
    y, z, head = position()
    core = lax.rem(head, 2)

    barrier = pltpu.get_barrier_semaphore()

    def greet(axis, step):
        pl.semaphore_signal(
            barrier, inc=1, device_id=shifted(y, z, head, axis, step), device_id_type=MESH
        )

    for axis in (0, 1):
        for step in (1, -1):
            greet(axis, step)

    @pl.when(core == 1)
    def _():
        greet(1, 2)
        greet(1, -2)

    loads = []
    for i in range(4):
        c = pltpu.make_async_copy(resp_ref.at[:, i], cache.at[i], load_sem.at[i])
        c.start()
        loads.append(c)
    pool_load = pltpu.make_async_copy(pool_ref, pool, pool_sem)
    pool_load.start()
    qall[y, z] = q_ref[...]
    picks = chosen(slot_ref, SYS_BLOCKS, (0, 1))

    @pl.when(core == 0)
    def _():
        pl.semaphore_wait(barrier, 4)

    @pl.when(core == 1)
    def _():
        pl.semaphore_wait(barrier, 6)

    def list_members():
        across = jnp.broadcast_to(map_ref[...].astype(F32), (HEAD, HEAD))
        task = jnp.transpose(across)
        row = lax.broadcasted_iota(jnp.int32, (HEAD, HEAD), 0)
        lane = lax.broadcasted_iota(jnp.int32, (HEAD, HEAD), 1)
        earlier = jnp.where((task == across) & (lane < row), 1.0, 0.0)
        rank = jnp.sum(earlier, axis=1, keepdims=True)
        spot = jnp.where(rank == lane.astype(F32), 1.0, 0.0).astype(BF16)
        mine = across[:16] == row[:16].astype(F32)
        ids = jnp.where(mine, lane[:16].astype(F32), 0.0).astype(BF16)
        count = jnp.sum(jnp.where(mine, 1.0, 0.0), axis=1, keepdims=True)
        table[...] = jnp.where(lane[:16] == HEAD - 1, count, dot(ids, spot)).astype(jnp.int32)

    def attend(i):
        loads[i].wait()
        length = len_ref[i]
        rows = slice(i * 16, (i + 1) * 16)

        none = jnp.zeros((16, HEAD), BF16)
        lhs = jnp.concatenate(
            [
                jnp.concatenate(
                    [q_ref[rows, cols(h)], none] if h < 2 else [none, q_ref[rows, cols(h)]], axis=1
                )
                for h in range(HEADS)
            ],
            axis=0,
        )
        p = weight_of(dot_t(lhs, inc_ref[0, i]))
        n = lax.rem(lax.broadcasted_iota(jnp.int32, p.shape, 0), 16)
        m = lax.broadcasted_iota(jnp.int32, p.shape, 1)
        p = jnp.where(m <= n, p, 0.0)
        total = jnp.zeros((64, HEAD), F32)
        own = jnp.sum(p, axis=1, keepdims=True)
        out = dot(p.astype(BF16), inc_ref[1, i])
        for part in range(4):
            keys = slice(part * 512, (part + 1) * 512)
            p = weight_of(dot_t(lhs, cache[i, 0, keys, :]))
            where = lax.broadcasted_iota(jnp.int32, p.shape, 1) + part * 512
            p = jnp.where(where < length, p, 0.0)
            total = total + lane_sum(p)
            out = out + dot(p.astype(BF16), cache[i, 1, keys, :])
        wide = jnp.broadcast_to(jnp.sum(total, axis=1, keepdims=True) + own, (64, HEAD))
        for h in range(HEADS):
            at = slice(h * 16, (h + 1) * 16)
            oloc[rows, cols(h)] = out[at, cols(h // 2)]
            lloc[rows, cols(h)] = wide[at]

    def copies(axis1):
        axis2 = 1 - axis1
        n1, n2 = (NY, NZ) if axis1 == 0 else (NZ, NY)
        c1, c2 = (y, z) if axis1 == 0 else (z, y)
        h1, h2 = n1 // 2, n2 // 2
        offsets = [0]
        for k in range(1, h1):
            offsets += [-k, k]
        offsets.append(h1)

        def piece(i1, i2, part):
            a, b = (i1, i2) if axis1 == 0 else (i2, i1)
            view = qall.at[a, b]
            return view if part is None else view.at[pl.ds(part * (ROWS // 2), ROWS // 2)]

        def first(d, k):
            s = 1 - 2 * d
            if h1 == 2:
                origin, by = k, 1
            else:
                origin, by = 2 * (k // 2), 1 + k % 2
            view = piece(wrap(c1 - s * origin, n1), c2, d if k == h1 - 1 else None)
            return pltpu.make_async_remote_copy(
                src_ref=view, dst_ref=view, send_sem=s1.at[d, k], recv_sem=r1.at[d, k],
                device_id=shifted(y, z, head, axis1, s * by), device_id_type=MESH,
            )

        def second(j, d, k):
            s = 1 - 2 * d
            view = piece(wrap(c1 + offsets[j], n1), wrap(c2 - s * k, n2), d if k == h2 - 1 else None)
            return pltpu.make_async_remote_copy(
                src_ref=view, dst_ref=view, send_sem=s2.at[d, j, k], recv_sem=r2.at[d, j, k],
                device_id=shifted(y, z, head, axis2, s), device_id_type=MESH,
            )

        def spread(j):
            for e in (0, 1):
                second(j, e, 0).start()

        def phase1(work):
            both = (0, 1)
            if h1 == 2:
                for d in both:
                    first(d, 0).start()
                spread(0)
                attend(work[0])
                for d in both:
                    first(d, 0).wait_recv()
                    first(d, 1).start()
                for d in both:
                    spread(1 + d)
                attend(work[1])
                for d in both:
                    first(d, 1).wait_recv()
                spread(n1 - 1)
            else:
                for k in (1, 0):
                    for d in both:
                        first(d, k).start()
                spread(0)
                attend(work[0])
                attend(work[1])
                for d in both:
                    first(d, 1).wait_recv()
                    first(d, 3).start()
                    first(d, 2).start()
                for d in both:
                    first(d, 0).wait_recv()
                    spread(1 + d)
                for d in both:
                    spread(3 + d)
            attend(work[2])
            attend(work[3])
            if h1 != 2:
                for d in both:
                    first(d, 2).wait_recv()
                    spread(5 + d)
                for d in both:
                    first(d, 3).wait_recv()
                spread(n1 - 1)

        def forward(k):
            for j in range(n1):
                for d in (0, 1):
                    second(j, d, k).wait_recv()
                    if k < h2 - 1:
                        second(j, d, k + 1).start()

        def drain():
            for k in range(h1):
                for d in (0, 1):
                    first(d, k).wait_send()
            for k in range(h2):
                for j in range(n1):
                    for d in (0, 1):
                        second(j, d, k).wait_send()

        return phase1, forward, drain

    def on(core_index, action):
        @pl.when(core == core_index)
        def _():
            action()

    def start0():
        copies(0)[0]((0, 1, 2, 3))
        list_members()

    def start1():
        copies(1)[0]((0, 1, 2, 3))
        list_members()

    on(0, start0)
    on(1, start1)
    pool_load.wait()

    q_store = pltpu.make_async_copy(qall, q_out, q_sem)

    def keep(at):
        return pltpu.make_async_copy(acc.at[at], acc_out.at[at], acc_sem.at[at])

    def compute(count, unit):
        def coords(m):
            u = unit + m // 4
            k = lax.div(u, 2)
            odd = lax.rem(u, 2)
            column = jnp.where(odd == 1, -1 - k, k)
            row = jnp.where(k == 1, -1, jnp.where(k == 2, 1, jnp.where(k == 3, 2, 0)))
            return (
                jnp.where(core == 0, m % 4, wrap(y + row, NY)),
                jnp.where(core == 0, wrap(z + column, NZ), odd * 4 + m % 4),
            )

        def load_q(m):
            return qall[coords(m)]

        def store(m, out, total):
            at = coords(m)
            acc[at] = out
            keep(at).start()
            sums[at] = jnp.concatenate([total, jnp.zeros((8, HEAD - ROWS), F32)], axis=1)

        system_round(count, load_q, store, pool, picks, qtmp, sbuf, otmp, lbuf)

    def in_round(r, index, core_index, action):
        @pl.when((r == index) & (core == core_index))
        def _():
            action()

    def one_round(r, _):
        @pl.when((r == 0) | (r == 4))
        def _():
            compute(4, jnp.where(r == 0, 0, 7))

        @pl.when((r > 0) & (r < 4))
        def _():
            compute(8, 2 * r - 1)

        for k in range(4):
            in_round(r, k, 0, lambda: copies(0)[1](k))
        in_round(r, 0, 1, lambda: copies(1)[1](0))
        in_round(r, 2, 1, lambda: copies(1)[1](1))

        @pl.when(r == 3)
        def _():
            q_store.start()

        return 0

    lax.fori_loop(0, 5, one_round, 0)
    on(0, lambda: copies(0)[2]())
    on(1, lambda: copies(1)[2]())
    for a in range(NY):
        for b in range(NZ):
            keep((a, b)).wait()
    q_store.wait()


def prefix_kernel(
    rc, slot_ref, table_ref, q_hbm, pool_hbm, lin_ref, acc_out, l_ref, sel,
    q_ref, pool_ref, acc, lanes, sbuf, qbuf, obuf, lbuf, system, item_slot, item_prompt, item_part, q_sem, pool_sem, acc_sem,
):
    q_load = pltpu.make_async_copy(q_hbm, q_ref, q_sem)
    q_load.start()
    pool_load = pltpu.make_async_copy(pool_hbm, pool_ref, pool_sem)
    pool_load.start()
    slots = slot_ref.shape[0]
    total_rows = q_ref.shape[0]
    chunks = total_rows // rc

    for i in range(8):
        system[i] = 0
    count = jnp.int32(0)
    items_p = jnp.int32(0)
    for i in range(slots):
        logical = slot_ref[i]
        system[count] = i
        count = count + (logical < SYS_BLOCKS).astype(jnp.int32)
        p = lax.div(jnp.maximum(logical - SYS_BLOCKS, 0), PROMPT_BLOCKS)
        n = jnp.where(logical < SYS_BLOCKS, 0, table_ref[p, HEAD - 1])
        for c in range(2):
            item_slot[items_p] = i
            item_prompt[items_p] = p
            item_part[items_p] = c
            items_p = items_p + (n > c * GROUP).astype(jnp.int32)
    count = jnp.maximum(count - 4, 0)

    def rows_of(c):
        return pl.ds(pl.multiple_of(c * rc, rc), rc)

    def score(item, h):
        c = lax.div(item, count)
        b = system[4 + lax.rem(item, count)]
        return dot_t(q_ref[rows_of(c), cols(h)], pool_ref[0, b, :, cols(h // 2)])

    acc[...] = jnp.zeros_like(acc)
    lanes[...] = jnp.zeros_like(lanes)
    q_load.wait()
    pool_load.wait()
    for n in range(2):
        for kv in range(2):
            sel[kv, n] = pool_ref[kv, system[2 + n]]

    @pl.when(count > 0)
    def _():
        items = count * chunks
        sbuf[0] = score(0, 0)

        def step(item, _):
            rows = rows_of(lax.div(item, count))
            turn = lax.rem(item, count)
            b = system[4 + turn]
            following = jnp.minimum(item + 1, items - 1)
            for h in range(HEADS):
                if h < HEADS - 1:
                    sbuf[(h + 1) % 2] = score(item, h + 1)
                else:
                    sbuf[0] = score(following, 0)
                p = weight_of(sbuf[h % 2])
                part = lane_sum(p)
                out = dot(p.astype(BF16), pool_ref[1, b, :, cols(h // 2)])
                lanes[rows, cols(h)] += part
                acc[rows, cols(h)] += out
            return 0

        lax.fori_loop(0, items, step, 0)

    rows_g = GROUP * 16

    def pick(k, turn):
        p = item_prompt[k]
        c = item_part[k]
        for m in range(GROUP):
            r = table_ref[p, c * GROUP + m]
            qbuf[turn, m * 16 : (m + 1) * 16, :] = q_ref[pl.ds(pl.multiple_of(r * 16, 16), 16), :]

    def member_score(k, turn, g):
        lhs = jnp.concatenate([qbuf[turn, :, cols(2 * g)], qbuf[turn, :, cols(2 * g + 1)]], axis=0)
        return dot_t(lhs, pool_ref[0, item_slot[k], :, cols(g)])

    def member_weights(k, g):
        w = weight_of(sbuf[g, : 2 * rows_g])
        part = lane_sum(w)
        out = dot(w.astype(BF16), pool_ref[1, item_slot[k], :, cols(g)])
        for j in range(2):
            at = slice(j * rows_g, (j + 1) * rows_g)
            obuf[:, cols(2 * g + j)] = out[at]
            lbuf[:, cols(2 * g + j)] = part[at]

    @pl.when(items_p > 0)
    def _():
        pick(0, 0)
        sbuf[0, : 2 * rows_g] = member_score(0, 0, 0)

        def one(k, _):
            turn = lax.rem(k, 2)
            following = jnp.minimum(k + 1, items_p - 1)
            sbuf[1, : 2 * rows_g] = member_score(k, turn, 1)
            pick(following, 1 - turn)
            member_weights(k, 0)
            sbuf[0, : 2 * rows_g] = member_score(following, 1 - turn, 0)
            member_weights(k, 1)
            p = item_prompt[k]
            c = item_part[k]
            n = table_ref[p, HEAD - 1]
            for m in range(GROUP):
                r = table_ref[p, c * GROUP + m]
                at = pl.ds(pl.multiple_of(r * 16, 16), 16)
                src = slice(m * 16, (m + 1) * 16)
                there = jnp.where(c * GROUP + m < n, 1.0, 0.0)
                acc[at, :] += obuf[src, :] * there
                lanes[at, :] += lbuf[src, :] * there
            return 0

        lax.fori_loop(0, items_p, one, 0)

    acc_store = pltpu.make_async_copy(acc, acc_out, acc_sem)
    acc_store.start()
    picker = head_picker()

    def finish(c, _):
        total = head_sums(picker, lanes[pl.ds(pl.multiple_of(c * 512, 512), 512), :])
        for m in range(8):
            l_ref[c * 8 + m] = lin_ref[c * 8 + m]
            l_ref[c * 8 + m, :, :ROWS] += total[:, m * ROWS : (m + 1) * ROWS]
        return 0

    lax.fori_loop(0, total_rows // 512, finish, 0)
    acc_store.wait()


def finish_kernel(
    slot_ref, l_ref, q_hbm, oloc, lloc, res_ref, pool, first_ref, second_ref, w_ref, down_ref, up_ref, gain_ref, vhw_ref,
    hid_ref, val_ref,
    q_ref, wbuf, acc, acc2, sums, far, qtmp, sbuf, otmp, lbuf, part1, lpart1, mine, pmine,
    rb_y, rb_z, rl_y, rl_z, rb2, rl2, chunk, rchunk, small, rsmall,
    q_sem, w_sem, a_sem, s1, r1, t1, u1, s2, r2, t2, u2, hs, hr, ss, sr,
):
    q_load = pltpu.make_async_copy(q_hbm, q_ref, q_sem)
    q_load.start()
    y, z, head = position()
    core = lax.rem(head, 2)
    seq = y * NZ + z
    barrier = pltpu.get_barrier_semaphore()

    def on(core_index, action):
        @pl.when(core == core_index)
        def _():
            action()

    def greet(to):
        pl.semaphore_signal(barrier, inc=1, device_id=to, device_id_type=MESH)

    def greet_axes(ring, direct, n):
        for step in (1, -1):
            greet(shifted(y, z, head, ring, step))
        for t in range(1, n):
            greet(shifted(y, z, head, direct, t))

    for t in range(1, NH):
        greet((seq, wrap(head + t, NH)))
    on(0, lambda: greet_axes(1, 0, NY))
    on(1, lambda: greet_axes(0, 1, NZ))
    parts = [
        pltpu.make_async_copy(first_ref, acc, a_sem.at[0]),
        pltpu.make_async_copy(second_ref, acc2, a_sem.at[1]),
    ]
    for x in parts:
        x.start()
    wcopy = pltpu.make_async_copy(w_ref, wbuf, w_sem)
    picks = [(n, v) for n, (_, v) in enumerate(chosen(slot_ref, SYS_BLOCKS, (2, 3)))]

    def compute(count, unit, arrived):
        def coords(m):
            u = unit + m // 4
            k = lax.div(u, 2)
            odd = lax.rem(u, 2)
            column = jnp.where(odd == 1, 3 - k, k - 4)
            row = jnp.where(k == 0, 2, jnp.where(k == 1, 1, jnp.where(k == 2, -1, 0)))
            place = jnp.where(odd == 0, FAR_FIRST[m % 4], FAR_FIRST[4 + m % 4])
            return (
                jnp.where(core == 0, m % 4, wrap(y + row, NY)),
                jnp.where(core == 0, wrap(z + column, NZ), wrap(z + place, NZ)),
            )

        def load_q(m):
            return q_ref[coords(m)]

        def store(m, out, total):
            at = coords(m)
            acc[at] = (acc[at] + acc2[at]) + out
            sums[at] = l_ref[at] + jnp.concatenate([total, jnp.zeros((8, HEAD - ROWS), F32)], axis=1)

        system_round(count, load_q, store, pool, picks, qtmp, sbuf, otmp, lbuf, arrived)

    half = ROWS // 2

    def ring(axis1):
        axis2 = 1 - axis1
        n1, n2 = (NY, NZ) if axis1 == 0 else (NZ, NY)
        c1, c2 = (y, z) if axis1 == 0 else (z, y)
        h = n1 // 2
        rb, rl = (rb_y, rl_y) if axis1 == 0 else (rb_z, rl_z)
        turns = sorted(range(1, n2), key=lambda t: -min(t, n2 - t)) + [0]
        order = [wrap(c2 + t, n2) for t in turns]

        def own(i, j):
            return acc[i, j] if axis1 == 0 else acc[j, i]

        def own_l(i):
            return sums.at[i] if axis1 == 0 else sums.at[:, i]

        def copy(d, k, j):
            if k == 0:
                src = far.at[j, pl.ds(d * half, half)]
                dst = rb.at[d, 0, j, pl.ds(d * half, half)]
            else:
                src = rb.at[d, k - 1, j]
                dst = rb.at[d, k, j]
            return pltpu.make_async_remote_copy(
                src_ref=src, dst_ref=dst, send_sem=s1.at[d, k, j], recv_sem=r1.at[d, k, j],
                device_id=shifted(y, z, head, axis1, 1 - 2 * d), device_id_type=MESH,
            )

        def copy_l(d, k):
            s = 1 - 2 * d
            src = own_l(wrap(c1 + s * (h - k), n1)) if k == d else rl.at[d, k - 1]
            return pltpu.make_async_remote_copy(
                src_ref=src, dst_ref=rl.at[d, k], send_sem=t1.at[d, k], recv_sem=u1.at[d, k],
                device_id=shifted(y, z, head, axis1, s), device_id_type=MESH,
            )

        def begin(js):
            for j in js:
                far[j] = own(wrap(c1 + h, n1), j).astype(BF16)
                for d in (0, 1):
                    copy(d, 0, j).start()

        def step_l(pairs):
            for d, k in pairs:
                if k > d:
                    copy_l(d, k - 1).wait_recv()
                    rl[d, k - 1] = rl[d, k - 1] + own_l(wrap(c1 + (1 - 2 * d) * (h - k), n1))[...]
                copy_l(d, k).start()

        def step(pairs, js):
            for j in js:
                for d, k in pairs:
                    copy(d, k - 1, j).wait_recv()
                    here = own(wrap(c1 + (1 - 2 * d) * (h - k), n1), j)
                    if k == 1:
                        a = pl.ds(d * half, half)
                        b = pl.ds((1 - d) * half, half)
                        there = rb[d, 0, j, a].astype(F32)
                        rb[d, 0, j, a] = (there + here[d * half : (d + 1) * half]).astype(BF16)
                        rb[d, 0, j, b] = here[(1 - d) * half : (2 - d) * half].astype(BF16)
                    else:
                        rb[d, k - 1, j] = (rb[d, k - 1, j].astype(F32) + here).astype(BF16)
                    copy(d, k, j).start()

        def direct(t):
            return pltpu.make_async_remote_copy(
                src_ref=part1.at[t], dst_ref=rb2.at[t], send_sem=s2.at[t], recv_sem=r2.at[t],
                device_id=shifted(y, z, head, axis2, t), device_id_type=MESH,
            )

        def direct_l(t):
            return pltpu.make_async_remote_copy(
                src_ref=lpart1.at[t], dst_ref=rl2.at[t], send_sem=t2.at[t], recv_sem=u2.at[t],
                device_id=shifted(y, z, head, axis2, t), device_id_type=MESH,
            )

        def final():
            for d in (0, 1):
                copy_l(d, h - 1).wait_recv()
            for t in turns:
                j = wrap(c2 + t, n2)
                at = (c1, j) if axis1 == 0 else (j, c1)
                v = sums[at] + rl[0, h - 1, j] + rl[1, h - 1, j]
                if t == 0:
                    small[...] = v
                else:
                    lpart1[t] = v
                    direct_l(t).start()
            for t in turns:
                j = wrap(c2 + t, n2)
                for d in (0, 1):
                    copy(d, h - 1, j).wait_recv()
                v = own(c1, j) + rb[0, h - 1, j].astype(F32) + rb[1, h - 1, j].astype(F32)
                if t == 0:
                    mine[...] = v
                else:
                    part1[t] = v.astype(BF16)
                    direct(t).start()
            w = small[...]
            for t in turns[:-1]:
                direct_l(t).wait_recv()
                w = w + rl2[t]
            small[...] = w
            v = mine[...]
            for t in turns[:-1]:
                direct(t).wait_recv()
                v = v + rb2[t].astype(F32)
            mine[...] = v

        def drain():
            for d in (0, 1):
                for k in range(h):
                    for j in order:
                        copy(d, k, j).wait_send()
                    if k >= d:
                        copy_l(d, k).wait_send()
            for t in turns[:-1]:
                direct(t).wait_send()
                direct_l(t).wait_send()

        return begin, step, step_l, final, drain, order

    def after0(r):
        begin, step, step_l, _, _, order = ring(1)
        if r == 0:
            pl.semaphore_wait(barrier, NH - 1 + 2 + NY - 1)
            step_l(((0, 0),))
            begin(order)
        else:
            step_l(((0, r), (1, r)))
            step(((0, r), (1, r)), order)

    def after1(r):
        begin, step, step_l, _, _, order = ring(0)
        a, b = order[:4], order[4:]
        if r == 0:
            pl.semaphore_wait(barrier, NH - 1 + 2 + NZ - 1)
            begin(a)
        elif r == 1:
            step_l(((0, 0),))
            begin(b)
            step(((0, 1),), a)
        elif r == 2:
            step_l(((0, 1),))
            step(((0, 1),), b)
            step(((1, 1),), a)
        else:
            step_l(((1, 1),))
            step(((1, 1),), b)

    def in_round(r, index, core_index, action):
        @pl.when((r == index) & (core == core_index))
        def _():
            action()

    q_load.wait()

    def arrived_in(r):
        @pl.when(r == 0)
        def _():
            for x in parts:
                x.wait()
            wcopy.start()

    def one_round(r, _):
        @pl.when((r == 0) | (r == 4))
        def _():
            compute(4, jnp.where(r == 0, 0, 7), lambda: arrived_in(r))

        @pl.when((r > 0) & (r < 4))
        def _():
            compute(8, 2 * r - 1, None)

        for k in range(4):
            in_round(r, k, 0, lambda: after0(k))
            in_round(r, k, 1, lambda: after1(k))
        return 0

    lax.fori_loop(0, 5, one_round, 0)
    on(0, lambda: ring(1)[3]())
    on(1, lambda: ring(0)[3]())

    rows_sum = jnp.transpose(jnp.concatenate([small[...], jnp.zeros((HEAD - 8, HEAD), F32)], axis=0))
    att = []
    for h in range(HEADS):
        den = rows_sum[:ROWS, h : h + 1] + lloc[:, cols(h)]
        att.append(((mine[:, cols(h)] + oloc[:, cols(h)]) / den).astype(BF16))
    att = jnp.concatenate(att, axis=1)
    low = dot_t(att, down_ref[...])
    low_hi = low.astype(BF16)
    low_lo = (low - low_hi.astype(F32)).astype(BF16)
    low_lo2 = (low - low_hi.astype(F32) - low_lo.astype(F32)).astype(BF16)
    low3 = jnp.concatenate([low_hi, low_lo, low_lo2], axis=1)
    wcopy.wait()
    def project(to):
        odd = lax.rem(to, 2)
        at = pl.ds(pl.multiple_of(to * CHUNK - odd * (HEAD // 2), HEAD), PADDED)
        u = up_ref[:, at]
        v = dot(att, wbuf[:, at]) + dot(low3, jnp.concatenate([u, u, u], axis=0))
        return jnp.where(odd == 1, v[:, HEAD // 2 :], v[:, :CHUNK])

    x_here = lax.div(head, 2)
    sends = []
    for t in (2, 1, 3, 0):
        chunk[t] = project(2 * wrap(x_here + t, NH // 2) + 1 - core).astype(BF16)
        x = pltpu.make_async_remote_copy(
            src_ref=chunk.at[t], dst_ref=rchunk.at[t], send_sem=hs.at[t], recv_sem=hr.at[t],
            device_id=(seq, 2 * x_here + 1 - core), device_id_type=MESH,
        )
        x.start()
        sends.append(x)
    across = {}
    for n, t in enumerate((2, 1, 3, 0)):
        v = project(2 * wrap(x_here + t, NH // 2) + core)
        sends[n].wait_recv()
        v = v + rchunk[t].astype(F32)
        if t == 0:
            pmine[...] = v
            continue
        chunk[3 + t] = v.astype(BF16)
        x = pltpu.make_async_remote_copy(
            src_ref=chunk.at[3 + t], dst_ref=rchunk.at[3 + t], send_sem=hs.at[3 + t], recv_sem=hr.at[3 + t],
            device_id=(seq, 2 * wrap(x_here + t, NH // 2) + core), device_id_type=MESH,
        )
        x.start()
        across[t] = x
        sends.append(x)
    p = pmine[...]
    for t in (1, 3, 2):
        across[t].wait_recv()
        p = p + rchunk[3 + t].astype(F32)

    res = res_ref[...].astype(F32)
    gain = gain_ref[...].reshape(1, CHUNK)
    vhw = vhw_ref[...].reshape(1, CHUNK)
    pg = p * gain
    terms = [p * p, res * res, res * pg, pg * pg, res * vhw, pg * vhw]
    lane = lax.broadcasted_iota(jnp.int32, (ROWS, HEAD), 1)
    packed = jnp.zeros((ROWS, HEAD), F32)
    for i, v in enumerate(terms):
        packed = jnp.where(lane == i, jnp.sum(v, axis=1, keepdims=True), packed)
    packed = jnp.concatenate([packed, jnp.zeros((HEAD - ROWS, HEAD), F32)], axis=0)
    small[...] = jnp.transpose(packed)[:8]
    sends2 = []
    for t in range(1, NH):
        x = pltpu.make_async_remote_copy(
            src_ref=small, dst_ref=rsmall.at[t - 1], send_sem=ss.at[t - 1], recv_sem=sr.at[t - 1],
            device_id=(seq, wrap(head + t, NH)), device_id_type=MESH,
        )
        x.start()
        sends2.append(x)
    total = small[...]
    for t in range(1, NH):
        sends2[t - 1].wait_recv()
        total = total + rsmall[t - 1]
    sq, res2, rpg, pg2, rw, pgw = [total[i : i + 1] for i in range(6)]
    r = lax.rsqrt(sq / MODEL_WIDTH + EPS)
    power = res2 + 2.0 * r * rpg + r * r * pg2
    value = (rw + r * pgw) * lax.rsqrt(power / MODEL_WIDTH + EPS)
    for i in range(4):
        val_ref[i : i + 1, :] = value[:, i * 16 : (i + 1) * 16]
    rcol = jnp.transpose(jnp.broadcast_to(r, (HEAD, HEAD)))[:ROWS, :1]
    hid_ref[...] = (res + pg * rcol).astype(BF16)
    for x in sends + sends2:
        x.wait_send()
    on(0, lambda: ring(1)[4]())
    on(1, lambda: ring(0)[4]())


def local(
    queries, incoming_key_value, prefix_key_value_pool, response_key_value, residual, lengths,
    rollout_task_map, slot_block_table, output_projection_weight, adapter_down_weight,
    adapter_up_weight, post_norm_gain, value_head_weight,
):
    vmem = pl.BlockSpec(memory_space=pltpu.VMEM)
    smem = pl.BlockSpec(memory_space=pltpu.SMEM)
    hbm = pl.BlockSpec(memory_space=pltpu.HBM)
    dma = pltpu.SemaphoreType.DMA
    sds = jax.ShapeDtypeStruct
    devices = NY * NZ
    rows_all = devices * ROWS
    pool_buf = pltpu.VMEM((2, 8, 512, 256), BF16)
    round_bufs = [
        pltpu.VMEM((8 * ROWS, WIDTH), BF16),
        pltpu.VMEM((2, 512, 512), F32),
        pltpu.VMEM((8 * ROWS, WIDTH), F32),
        pltpu.VMEM((8 * ROWS, WIDTH), F32),
    ]

    qall, acc, sums, oloc, lloc, table = pl.pallas_call(
        gather_kernel,
        out_shape=(
            sds((NY, NZ, ROWS, WIDTH), BF16),
            sds((NY, NZ, ROWS, WIDTH), F32),
            sds((NY, NZ, 8, HEAD), F32),
            sds((ROWS, WIDTH), F32),
            sds((ROWS, WIDTH), F32),
            sds((16, HEAD), jnp.int32),
        ),
        in_specs=[smem, smem, vmem, vmem, vmem, hbm, hbm],
        out_specs=(hbm, hbm, vmem, vmem, vmem, vmem),
        scratch_shapes=[
            pltpu.VMEM((NY, NZ, ROWS, WIDTH), BF16),
            pltpu.VMEM((4, 2, 2048, 256), BF16),
            pool_buf,
            pltpu.VMEM((NY, NZ, ROWS, WIDTH), F32),
            *round_bufs,
            dma((4,)),
            dma(()),
            dma(()),
            dma((NY, NZ)),
            dma((2, NZ // 2)),
            dma((2, NZ // 2)),
            dma((2, NZ, NZ // 2)),
            dma((2, NZ, NZ // 2)),
        ],
        compiler_params=pltpu.CompilerParams(
            collective_id=0, has_side_effects=True, vmem_limit_bytes=K1_MIB * MIB
        ),
        name="gather_queries",
    )(
        lengths, slot_block_table, queries.reshape(ROWS, WIDTH), incoming_key_value,
        rollout_task_map.reshape(1, -1), response_key_value, prefix_key_value_pool,
    )

    rc = 1024
    acc2, sums2, chosen_blocks = pl.pallas_call(
        functools.partial(prefix_kernel, rc),
        out_shape=(
            sds((rows_all, WIDTH), F32),
            sds((devices, 8, HEAD), F32),
            sds((2, 2, 512, 256), BF16),
        ),
        in_specs=[smem, smem, hbm, hbm, vmem],
        out_specs=(hbm, vmem, vmem),
        scratch_shapes=[
            pltpu.VMEM((rows_all, WIDTH), BF16),
            pool_buf,
            pltpu.VMEM((rows_all, WIDTH), F32),
            pltpu.VMEM((rows_all, WIDTH), F32),
            pltpu.VMEM((2, rc, 512), F32),
            pltpu.VMEM((2, GROUP * 16, WIDTH), BF16),
            pltpu.VMEM((GROUP * 16, WIDTH), F32),
            pltpu.VMEM((GROUP * 16, WIDTH), F32),
            pltpu.SMEM((16,), jnp.int32),
            pltpu.SMEM((24,), jnp.int32),
            pltpu.SMEM((24,), jnp.int32),
            pltpu.SMEM((24,), jnp.int32),
            dma(()),
            dma(()),
            dma(()),
        ],
        compiler_params=pltpu.CompilerParams(vmem_limit_bytes=K2_MIB * MIB),
        name="prefix_attention",
    )(
        slot_block_table, table, qall.reshape(rows_all, WIDTH), prefix_key_value_pool,
        sums.reshape(devices, 8, HEAD),
    )

    hidden, values = pl.pallas_call(
        finish_kernel,
        out_shape=(sds((ROWS, CHUNK), BF16), sds((4, 16), F32)),
        in_specs=[smem, vmem, hbm] + [vmem] * 4 + [hbm] * 3 + [vmem] * 4,
        out_specs=(vmem, vmem),
        scratch_shapes=[
            pltpu.VMEM((NY, NZ, ROWS, WIDTH), BF16),
            pltpu.VMEM((WIDTH, MODEL_WIDTH), BF16),
            pltpu.VMEM((NY, NZ, ROWS, WIDTH), F32),
            pltpu.VMEM((NY, NZ, ROWS, WIDTH), F32),
            pltpu.VMEM((NY, NZ, 8, HEAD), F32),
            pltpu.VMEM((NZ, ROWS, WIDTH), BF16),
            *round_bufs,
            pltpu.VMEM((NZ, ROWS, WIDTH), BF16),
            pltpu.VMEM((NZ, 8, HEAD), F32),
            pltpu.VMEM((ROWS, WIDTH), F32),
            pltpu.VMEM((ROWS, CHUNK), F32),
            pltpu.VMEM((2, NY // 2, NZ, ROWS, WIDTH), BF16),
            pltpu.VMEM((2, NZ // 2, NY, ROWS, WIDTH), BF16),
            pltpu.VMEM((2, NY // 2, NZ, 8, HEAD), F32),
            pltpu.VMEM((2, NZ // 2, NY, 8, HEAD), F32),
            pltpu.VMEM((NZ, ROWS, WIDTH), BF16),
            pltpu.VMEM((NZ, 8, HEAD), F32),
            pltpu.VMEM((NH - 1, ROWS, CHUNK), BF16),
            pltpu.VMEM((NH - 1, ROWS, CHUNK), BF16),
            pltpu.VMEM((8, HEAD), F32),
            pltpu.VMEM((NH - 1, 8, HEAD), F32),
            dma(()),
            dma(()),
            dma((2,)),
            dma((2, NZ // 2, NZ)),
            dma((2, NZ // 2, NZ)),
            dma((2, NZ // 2)),
            dma((2, NZ // 2)),
            dma((NZ,)),
            dma((NZ,)),
            dma((NZ,)),
            dma((NZ,)),
            dma((NH - 1,)),
            dma((NH - 1,)),
            dma((NH - 1,)),
            dma((NH - 1,)),
        ],
        compiler_params=pltpu.CompilerParams(
            collective_id=1, has_side_effects=True, vmem_limit_bytes=K3_MIB * MIB
        ),
        name="reduce_and_project",
    )(
        slot_block_table, sums2.reshape(NY, NZ, 8, HEAD), qall, oloc, lloc,
        residual.reshape(ROWS, CHUNK), chosen_blocks, acc, acc2.reshape(NY, NZ, ROWS, WIDTH),
        output_projection_weight,
        adapter_down_weight.T, adapter_up_weight, post_norm_gain, value_head_weight,
    )
    return hidden.reshape(residual.shape), values


def solution(mesh):
    placed = (
        P("seq", None, "head"),
        P(None, "seq", None, "head"),
        P(None, "seq", None, "head"),
        P(None, "seq", None, "head"),
        P("seq", None, "head"),
        P("seq"),
        P(),
        P("seq"),
        P("head", None),
        P("head", None),
        P(),
        P("head"),
        P("head"),
    )
    return jax.shard_map(
        local,
        mesh=mesh,
        in_specs=placed,
        out_specs=(P("seq", None, "head"), P("seq", None)),
        check_vma=False,
    )
```
